128 devices in a mesh: sx: 8 (over x_lo, z), sy: 16 (over y, x_hi, core).
Axes of the slice: x: 4 (x_hi: 2, x_lo: 2; x = x_hi * 2 + x_lo), y: 4, z: 4, core: 2. Of those that a mesh axis runs over, the one named last changes fastest.
Arguments:
- wave: bfloat16 [16, 128, 64, 512], P('sx', 'sy'), may hold values from -8 to 8
- potential: float32 [16, 128, 64], P('sx', 'sy'), may hold values from 0 to 2
- lower_cut: float32 [1], replicated, may hold values from 0.8 to 1.6
- upper_edge: float32 [1], replicated, may hold values from 5 to 6
Outputs:
- margin: float32 [512, 512], P('sy')
- projected: float32 [512, 512], P('sy')
The draws below stay inside these ranges and needn't reach their ends.
All inputs are finite; a program needn't handle non-finite values.
Results may differ from the reference program's by a relative error of at most 0.0049.
Values may be sent and summed in bfloat16 or wider, within the bound.
A program may use at most 64 MiB of HBM per device.

```python
import math
import jax
import jax.numpy as jnp
from jax import lax

C = 512
NZ = 64
STEPS = 4
NX = 16
NY = 128


def draw_wave(key, part):
    key = jax.random.fold_in(key, 11)
    first_key, second_key = jax.random.split(key, 2)
    shape = (NX, NY, NZ, C)
    base = jax.random.normal(first_key, shape, jnp.float32)
    mixed = (base + 0.6 * jnp.roll(base, 1, axis=3) + 0.4 * jnp.roll(base, 2, axis=3)) / 1.3
    scales = jnp.exp(jax.random.uniform(second_key, (C,), jnp.float32, math.log(0.5), math.log(3.0)))
    return jnp.clip(mixed * scales, -8.0, 8.0).astype(jnp.bfloat16)


def level_of(rng, dims, pieces, least, top_value):
    def one(axis_at, parts):
        steps = jax.random.uniform(jax.random.fold_in(jax.random.fold_in(rng, 6), axis_at), (parts,), jnp.float32, least / len(pieces), top_value / len(pieces))
        return jnp.repeat(jnp.exp(steps), dims[axis_at] // parts).reshape((-1,) + (1,) * (len(dims) - axis_at - 1))

    factor_of = one(*pieces[0])
    for cut in pieces[1:]:
        factor_of = factor_of * one(*cut)
    return factor_of


def setup_inputs(seed: int = 0) -> dict:
    splits = jax.random.split(jax.random.key(seed), 5)
    return {
        "wave": draw_wave(jax.random.fold_in(splits[4], 71), 0),
        "potential": jnp.clip(2.0 * jax.random.uniform(splits[1], (NX, NY, NZ), jnp.float32) ** level_of(splits[1], (NX, NY, NZ), ((0, 8), (1, 16)), -0.2, 0.2), 0.0, 2.0),
        "lower_cut": jnp.clip(jax.random.uniform(splits[2], (1,), jnp.float32, 0.8, 1.6), 0.8, 1.6),
        "upper_edge": jnp.clip(jax.random.uniform(splits[3], (1,), jnp.float32, 5.0, 6.0), 5.0, 6.0),
    }


def mass_line(field, axis):
    extent = field.shape[axis]
    below = lax.slice_in_dim(field, 0, extent - 2, axis=axis)
    middle = lax.slice_in_dim(field, 1, extent - 1, axis=axis)
    above = lax.slice_in_dim(field, 2, extent, axis=axis)
    return (4.0 * middle + below + above) / 6.0


def stiff_line(field, axis):
    extent = field.shape[axis]
    below = lax.slice_in_dim(field, 0, extent - 2, axis=axis)
    middle = lax.slice_in_dim(field, 1, extent - 1, axis=axis)
    above = lax.slice_in_dim(field, 2, extent, axis=axis)
    return 2.0 * middle - below - above


def operate(padded, potential):
    zpadded = jnp.pad(padded, ((0, 0), (0, 0), (1, 1), (0, 0)))
    mass_z = mass_line(zpadded, 2)
    stiff_z = stiff_line(zpadded, 2)
    first = stiff_line(mass_line(mass_z, 1), 0)
    second = mass_line(stiff_line(mass_z, 1), 0)
    third = mass_line(mass_line(stiff_z, 1), 0)
    centre_field = padded[1:-1, 1:-1]
    return 0.5 * (first + second + third) + potential[..., None] * centre_field


def chebyshev(block, potential, lower_cut, upper_edge):
    centre = 0.5 * (upper_edge[0] + lower_cut[0])
    radius = 0.5 * (upper_edge[0] - lower_cut[0])

    def apply_field(field):
        return operate(jnp.pad(field.astype(jnp.float32), ((1, 1), (1, 1), (0, 0), (0, 0))), potential)

    previous = block
    current = ((apply_field(block) - centre * block.astype(jnp.float32)) / radius).astype(jnp.bfloat16)
    for _ in range(STEPS - 1):
        following = 2.0 * (apply_field(current) - centre * current.astype(jnp.float32)) / radius
        following = (following - previous.astype(jnp.float32)).astype(jnp.bfloat16)
        previous, current = current, following
    image = apply_field(current).astype(jnp.bfloat16)
    return current, image


def product(left, right):
    return lax.dot_general(left, right, (((0,), (0,)), ((), ())), preferred_element_type=jnp.float32)


def reference(wave, potential, lower_cut, upper_edge):
    width_block = math.gcd(C, 128)
    nblocks = C // width_block
    blocks = jnp.moveaxis(wave.reshape(NX, NY, NZ, nblocks, width_block), 3, 0)
    filtered, images = lax.map(lambda single: chebyshev(single, potential, lower_cut, upper_edge), blocks)
    nodes = NX * NY * NZ
    flat_f = filtered.reshape(nblocks, nodes, width_block)
    flat_i = images.reshape(nblocks, nodes, width_block)
    margin = jnp.concatenate([jnp.concatenate([product(flat_f[row_block], flat_f[column_block]) for column_block in range(nblocks)], axis=1) for row_block in range(nblocks)], axis=0)
    projected = jnp.concatenate([jnp.concatenate([product(flat_f[row_block], flat_i[column_block]) for column_block in range(nblocks)], axis=1) for row_block in range(nblocks)], axis=0)
    return margin / nodes, projected / nodes
```

```python
import functools

import jax
import jax.numpy as jnp
import numpy as np
from jax import lax
from jax.experimental import pallas as pl
from jax.experimental.pallas import tpu as pltpu
from jax.sharding import PartitionSpec as P

MESH = pl.DeviceIdType.MESH
F32, BF16 = jnp.float32, jnp.bfloat16
GROUP = 32
NT = (((1,), (1,)), ((), ()))


def stencil_matrix():
    my, ky = np.zeros((4, 6)), np.zeros((4, 6))
    for i in range(4):
        my[i, i : i + 3] = 1, 4, 1
        ky[i, i : i + 3] = -1, 2, -1
    mz, kz = np.zeros((64, 64)), np.zeros((64, 64))
    for i in range(64):
        for j in range(max(i - 1, 0), min(i + 2, 64)):
            mz[i, j] = 4 if i == j else 1
            kz[i, j] = 2 if i == j else -1
    m = np.einsum("ij,kl->jlik", my, mz).reshape(6, 64, 256)
    g = np.einsum("ij,kl->jlik", ky, mz) + np.einsum("ij,kl->jlik", my, kz)
    g = g.reshape(6, 64, 256)
    p, q = 2 * m + 4 * g, g - m
    own = lambda t: t[1:5].reshape(256, 256)
    edge = lambda t: np.concatenate([t[5], t[0]], axis=0)
    return np.concatenate([own(p), own(q), own(q), edge(p), edge(q), edge(q)], axis=0)


def peer(k, z, x, c):
    dz, dx, dc = k % 4, (k // 4) % 4, k // 16
    sz = dz + c * (4 - 2 * dz)
    sx = dx + c * (4 - 2 * dx)
    return (z + sz) % 4, (x + sx) % 4, (c + dc) % 2


def source(k, z, x, c):
    dz, dx, dc = k % 4, (k // 4) % 4, k // 16
    cs = (c + dc) % 2
    sz = dz + cs * (4 - 2 * dz)
    sx = dx + cs * (4 - 2 * dx)
    return (z + 4 - sz % 4) % 4, (x + 4 - sx % 4) % 4, cs


def kernel(
    wave, pot, low, high, w_in, margin, projected,
    t, u0, u1, u2, u3, u4, img, d0, rf, ri, gm, part, other, half, rs, ob,
    in_s, in_r, pin_s, pin_r, hal_s, hal_r, phal_s, phal_r, edge_s, edge_r,
    f_s, f_r, i_s, i_r, core_s, core_r, rs_s, rs_r, ag_s, ag_r,
):
    sx, sy = lax.axis_index("sx"), lax.axis_index("sy")
    z, x = sx % 4, 2 * ((sy // 2) % 2) + sx // 4
    yy, c = sy // 4, sy % 2
    s4 = sy % 4
    j = sx * 4 + s4

    def mesh_id(zz, xx, cc, y):
        return ((xx % 2) * 4 + zz, y * 4 + (xx // 2) * 2 + cc)

    def index(zz, xx, cc):
        return ((xx % 2) * 4 + zz) * 4 + (xx // 2) * 2 + cc

    def remote(src, dst, ss, rr, dev):
        return pltpu.make_async_remote_copy(
            src_ref=src, dst_ref=dst, send_sem=ss, recv_sem=rr, device_id=dev, device_id_type=MESH
        )

    for u in (u0, u1, u2, u3, u4):
        u[0] = jnp.zeros(u.shape[1:], BF16)
        u[17] = jnp.zeros(u.shape[1:], BF16)
        for b in (0, 1, 10, 11):
            u[:, b] = jnp.zeros((18, 16, 256), BF16)
    d0[:, 0] = jnp.zeros((16, 1, 256), F32)
    d0[:, 9] = jnp.zeros((16, 1, 256), F32)

    barrier = pltpu.get_barrier_semaphore()

    @pl.loop(1, GROUP)
    def _(k):
        pl.semaphore_signal(
            barrier, inc=1, device_id=mesh_id(*peer(k, z, x, c), yy), device_id_type=MESH
        )

    for dy in (1, 2, 3):
        pl.semaphore_signal(
            barrier, inc=1, device_id=mesh_id(z, x, c, (yy + dy) % 4), device_id_type=MESH
        )

    eye = (
        lax.broadcasted_iota(jnp.int32, (256, 256), 0)
        == lax.broadcasted_iota(jnp.int32, (256, 256), 1)
    ).astype(F32).astype(BF16)
    for a in range(2):
        for b in range(2):
            nodes = wave[a, 4 * b : 4 * b + 4].reshape(256, 512)
            for h in range(2):
                t[a, b, 256 * h : 256 * h + 256] = lax.dot_general(
                    eye, nodes[:, 256 * h : 256 * h + 256], NT, preferred_element_type=F32
                ).astype(BF16)
            d0[2 * sx + a, 1 + 2 * s4 + b] = jnp.concatenate(
                [pot[a, 4 * b + i : 4 * b + i + 1, :] for i in range(4)], axis=1
            )

    pl.semaphore_wait(barrier, GROUP - 1 + 3)

    xs = pl.ds(1 + 2 * sx, 2)
    bs = pl.ds(2 + 2 * s4, 2)
    own_pot = d0.at[pl.ds(2 * sx, 2), pl.ds(1 + 2 * s4, 2)]

    def cols(i):
        return pl.ds(pl.multiple_of(16 * i, 16), 16)

    def in_copies(k):
        pz, px, pc = peer(k, z, x, c)
        dev = mesh_id(pz, px, pc, yy)
        rows = cols(index(pz, px, pc))
        return (
            remote(t.at[:, :, rows], u0.at[xs, bs], in_s.at[k], in_r.at[k], dev),
            remote(own_pot, own_pot, pin_s.at[k], pin_r.at[k], dev),
        )

    @pl.loop(1, GROUP)
    def _(k):
        for copy in in_copies(k):
            copy.start()

    u0[xs, bs] = t[:, :, cols(j)]

    def edge_copies(side, s):
        far = (yy + 3 + 2 * side) % 4
        mine, theirs = (2, 10) if side == 0 else (9, 1)
        dev = mesh_id(z, x, c, far)
        px = pl.ds(2 * s, 2)
        ux = pl.ds(1 + 2 * s, 2)
        return (
            remote(u0.at[ux, mine], u0.at[ux, theirs], hal_s.at[side, s], hal_r.at[side, s], dev),
            remote(
                d0.at[px, mine - 1], d0.at[px, theirs - 1],
                phal_s.at[side, s], phal_r.at[side, s], dev,
            ),
        )

    def send_on(s, quarter):
        @pl.when(jnp.logical_and(quarter == 0, yy > 0))
        def _():
            for copy in edge_copies(0, s):
                copy.start()

        @pl.when(jnp.logical_and(quarter == 3, yy < 3))
        def _():
            for copy in edge_copies(1, s):
                copy.start()

    send_on(sx, s4)

    @pl.loop(1, GROUP)
    def _(k):
        for copy in in_copies(k):
            copy.wait_recv()
        pz, px, pc = source(k, z, x, c)
        send_on((px % 2) * 4 + pz, (px // 2) * 2 + pc)

    centre = 0.5 * (high[0] + low[0])
    inv_radius = 1.0 / (0.5 * (high[0] - low[0]))

    def stencil(u, x0, lo, hi):
        n = hi - lo
        rows = 4 * n * 16
        own, edge = [], []
        for dx in (1, 0, 2):
            px = pl.ds(x0 + dx, 4)
            own.append(u[px, lo:hi].reshape(rows, 256))
            nxt = u[px, lo + 1 : hi + 1, :, 0:128].reshape(rows, 128)
            prv = u[px, lo - 1 : hi - 1, :, 128:256].reshape(rows, 128)
            first = lax.broadcasted_iota(jnp.int32, (rows, 128), 1) < 64
            edge.append(jnp.where(first, nxt, prv))
        lhs = jnp.concatenate(own + edge, axis=1)
        acc = jnp.dot(lhs, w_in[...], preferred_element_type=F32)
        return acc.reshape(4, n, 16, 256)

    def apply_step(u, prev, out, lo, hi):
        @pl.loop(0, 4)
        def _(i):
            x0 = 4 * i
            acc = stencil(u, x0, lo, hi)
            px = pl.ds(x0 + 1, 4)
            v = u[px, lo:hi].astype(F32)
            d = (d0[pl.ds(x0, 4), lo - 1 : hi - 1] - centre) * inv_radius
            if prev is None:
                res = acc * (inv_radius / 72.0) + d * v
            else:
                res = acc * (inv_radius / 36.0) + (2.0 * d) * v - prev[px, lo:hi].astype(F32)
            out[px, lo:hi] = res.astype(BF16)

    def outside_zero(out):
        @pl.when(yy == 0)
        def _():
            out[:, 1] = jnp.zeros((18, 16, 256), BF16)

        @pl.when(yy == 3)
        def _():
            out[:, 10] = jnp.zeros((18, 16, 256), BF16)

    apply_step(u0, None, u1, 3, 9)

    def halo_wait(side):
        for s in range(8):
            for copy in edge_copies(side, s):
                copy.wait_recv()

    @pl.when(yy < 3)
    def _():
        halo_wait(0)

    @pl.when(yy > 0)
    def _():
        halo_wait(1)

    apply_step(u0, None, u1, 1, 3)
    apply_step(u0, None, u1, 9, 11)
    outside_zero(u1)
    apply_step(u1, u0, u2, 1, 11)
    outside_zero(u2)
    apply_step(u2, u1, u3, 1, 11)
    outside_zero(u3)
    apply_step(u3, u2, u4, 2, 10)

    def layer(side):
        far = (yy + 3 + 2 * side) % 4
        mine, theirs, lanes = (2, 10, pl.ds(0, 128)) if side == 0 else (9, 1, pl.ds(128, 128))
        return remote(
            u4.at[pl.ds(1, 16), mine, :, lanes],
            u4.at[pl.ds(1, 16), theirs, :, lanes],
            edge_s.at[side], edge_r.at[side], mesh_id(z, x, c, far),
        )

    @pl.when(yy > 0)
    def _():
        layer(0).start()

    @pl.when(yy < 3)
    def _():
        layer(1).start()

    def out_copy(k, src, dst, ss, rr, first):
        pz, px, pc = peer(k, z, x, c)
        i = index(pz, px, pc)
        return remote(
            src.at[pl.ds(first + 2 * (i // 4), 2), pl.ds(2 * first + 2 * (i % 4), 2)],
            dst.at[:, :, cols(j)], ss.at[k], rr.at[k], mesh_id(pz, px, pc, yy),
        )

    @pl.loop(1, GROUP)
    def _(k):
        out_copy(k, u4, rf, f_s, f_r, 1).start()

    rf[:, :, cols(j)] = u4[xs, bs]

    @pl.when(yy < 3)
    def _():
        layer(0).wait_recv()

    @pl.when(yy > 0)
    def _():
        layer(1).wait_recv()

    @pl.loop(0, 4)
    def _(i):
        x0 = 4 * i
        acc = stencil(u4, x0, 2, 10)
        v = u4[pl.ds(x0 + 1, 4), 2:10].astype(F32)
        res = acc * (1.0 / 72.0) + d0[pl.ds(x0, 4), 1:9] * v
        img[pl.ds(x0, 4)] = res.astype(BF16)

    @pl.loop(1, GROUP)
    def _(k):
        out_copy(k, img, ri, i_s, i_r, 0).start()

    ri[:, :, cols(j)] = img[pl.ds(2 * sx, 2), pl.ds(2 * s4, 2)]

    def core_copy(n):
        return remote(
            part.at[n, :, 1 - c], other.at[n], core_s.at[n], core_r.at[n], (sx, sy + 1 - 2 * c)
        )

    def gram(n, right):
        whole = jnp.concatenate([rf[a, b] for a in range(2) for b in range(2)], axis=1)
        with_ = jnp.concatenate([right[a, b] for a in range(2) for b in range(2)], axis=1)
        for r in range(4):
            g = lax.dot_general(
                whole[128 * r : 128 * r + 128], with_, NT, preferred_element_type=F32
            ).reshape(2, 2, 2, 16, 512)
            gm[2 * r : 2 * r + 2] = g
            part[n, 2 * r : 2 * r + 2] = g.astype(BF16)
        core_copy(n).start()

    def rs_peer(k):
        dz, dx, dy = k % 4, (k // 4) % 4, k // 16
        tz = (z + dz + c * (4 - 2 * dz)) % 4
        tx = (x + dx + c * (4 - 2 * dx)) % 4
        ty = (yy + dy + c * (4 - 2 * dy)) % 4
        return mesh_id(tz, tx, c, ty)

    def rs_copy(n, k):
        dx, dy = rs_peer(k)
        return remote(
            half.at[n, dy // 2, dx // 4, :, pl.ds(pl.multiple_of(128 * (dx % 4), 128), 128)],
            rs.at[n, k], rs_s.at[n, k], rs_r.at[n, k], (dx, dy),
        )

    def scatter(n):
        core_copy(n).wait_recv()
        half[n] = (gm[:, c] + other[n].astype(F32)).astype(BF16)

        @pl.loop(1, 64)
        def _(k):
            rs_copy(n, k).start()

        rs[n, 0] = half[n, sy // 2, sx // 4, :, pl.ds(pl.multiple_of(128 * (sx % 4), 128), 128)]

    def collect(n):
        @pl.loop(1, 64)
        def _(k):
            rs_copy(n, k).wait_recv()

        ob[sx, n] = jnp.sum(rs[n].astype(F32), axis=0) * (1.0 / 131072.0)

    @pl.loop(1, GROUP)
    def _(k):
        out_copy(k, u4, rf, f_s, f_r, 1).wait_recv()

    gram(0, rf)
    scatter(0)

    @pl.loop(1, GROUP)
    def _(k):
        out_copy(k, img, ri, i_s, i_r, 0).wait_recv()

    gram(1, ri)
    scatter(1)
    collect(0)
    collect(1)

    def ag_copy(k):
        return remote(ob.at[sx], ob.at[sx], ag_s.at[k], ag_r.at[k], ((sx + k) % 8, sy))

    for k in range(1, 8):
        ag_copy(k).start()

    @pl.loop(1, GROUP)
    def _(k):
        for copy in in_copies(k):
            copy.wait_send()
        out_copy(k, u4, rf, f_s, f_r, 1).wait_send()
        out_copy(k, img, ri, i_s, i_r, 0).wait_send()

    def sent(s, quarter):
        @pl.when(jnp.logical_and(quarter == 0, yy > 0))
        def _():
            for copy in edge_copies(0, s):
                copy.wait_send()

        @pl.when(jnp.logical_and(quarter == 3, yy < 3))
        def _():
            for copy in edge_copies(1, s):
                copy.wait_send()

    @pl.loop(0, 8)
    def _(s):
        sent(s, 0)
        sent(s, 3)

    @pl.when(yy > 0)
    def _():
        layer(0).wait_send()

    @pl.when(yy < 3)
    def _():
        layer(1).wait_send()

    for n in range(2):
        core_copy(n).wait_send()

        @pl.loop(1, 64)
        def _(k):
            rs_copy(n, k).wait_send()

    for k in range(1, 8):
        ag_copy(k).wait()
    for s in range(8):
        rows, lanes = pl.ds(16 * (s // 4), 16), pl.ds(128 * (s % 4), 128)
        margin[rows, lanes] = ob[s, 0]
        projected[rows, lanes] = ob[s, 1]


def on_device(wave, potential, lower_cut, upper_edge):
    dma = pltpu.SemaphoreType.DMA
    field = pltpu.VMEM((18, 12, 16, 256), BF16)
    block = pltpu.VMEM((2, 2, 512, 256), BF16)
    vmem = pl.BlockSpec(memory_space=pltpu.VMEM)
    smem = pl.BlockSpec(memory_space=pltpu.SMEM)
    weights = jnp.asarray(stencil_matrix(), BF16)
    return pl.pallas_call(
        kernel,
        out_shape=[jax.ShapeDtypeStruct((32, 512), F32)] * 2,
        in_specs=[vmem, vmem, smem, smem, vmem],
        out_specs=[vmem, vmem],
        scratch_shapes=[
            block,
            field, field, field, field, field,
            pltpu.VMEM((16, 8, 16, 256), BF16),
            pltpu.VMEM((16, 10, 1, 256), F32),
            block, block,
            pltpu.VMEM((8, 2, 2, 16, 512), F32),
            pltpu.VMEM((2, 8, 2, 2, 16, 512), BF16),
            pltpu.VMEM((2, 8, 2, 16, 512), BF16),
            pltpu.VMEM((2, 8, 2, 16, 512), BF16),
            pltpu.VMEM((2, 64, 16, 128), BF16),
            pltpu.VMEM((8, 2, 16, 128), F32),
            dma((32,)), dma((32,)), dma((32,)), dma((32,)),
            dma((2, 8)), dma((2, 8)), dma((2, 8)), dma((2, 8)),
            dma((2,)), dma((2,)),
            dma((32,)), dma((32,)), dma((32,)), dma((32,)),
            dma((2,)), dma((2,)),
            dma((2, 64)), dma((2, 64)),
            dma((8,)), dma((8,)),
        ],
        compiler_params=pltpu.CompilerParams(
            collective_id=0, has_side_effects=True, vmem_limit_bytes=48 << 20
        ),
    )(wave, potential, lower_cut, upper_edge, weights)


def solution(mesh):
    return jax.shard_map(
        on_device,
        mesh=mesh,
        in_specs=(P("sx", "sy", None, None), P("sx", "sy", None), P(), P()),
        out_specs=(P("sy", None), P("sy", None)),
        check_vma=False,
    )
```

```python
import functools

import jax
import jax.numpy as jnp
import numpy as np
from jax import lax
from jax.experimental import pallas as pl
from jax.experimental.pallas import tpu as pltpu
from jax.sharding import PartitionSpec as P

MESH = pl.DeviceIdType.MESH
F32, BF16 = jnp.float32, jnp.bfloat16
GROUP = 32
NT = (((1,), (1,)), ((), ()))


def stencil_matrix():
    my, ky = np.zeros((4, 6)), np.zeros((4, 6))
    for i in range(4):
        my[i, i : i + 3] = 1, 4, 1
        ky[i, i : i + 3] = -1, 2, -1
    mz, kz = np.zeros((64, 64)), np.zeros((64, 64))
    for i in range(64):
        for j in range(max(i - 1, 0), min(i + 2, 64)):
            mz[i, j] = 4 if i == j else 1
            kz[i, j] = 2 if i == j else -1
    m = np.einsum("ij,kl->jlik", my, mz).reshape(6, 64, 256)
    g = np.einsum("ij,kl->jlik", ky, mz) + np.einsum("ij,kl->jlik", my, kz)
    g = g.reshape(6, 64, 256)
    p, q = 2 * m + 4 * g, g - m
    own = lambda t: t[1:5].reshape(256, 256)
    edge = lambda t: np.concatenate([t[5], t[0]], axis=0)
    return np.concatenate([own(p), own(q), own(q), edge(p), edge(q), edge(q)], axis=0)


def kernel(
    wave_hbm, pot_hbm, low, high, w_hbm, margin, projected,
    wave, pot, w_in, t, u0, u1, u2, u3, u4, img, d0, rf, ri, gm, part, other, half, rs, ob,
    load, in_s, in_r, pin_s, pin_r, hal_s, hal_r, phal_s, phal_r, edge_s, edge_r,
    f_s, f_r, i_s, i_r, core_s, core_r, rs_s, rs_r, ag_s, ag_r,
):
    loads = [
        pltpu.make_async_copy(src, dst, load.at[i])
        for i, (src, dst) in enumerate([(wave_hbm, wave), (pot_hbm, pot), (w_hbm, w_in)])
    ]
    for copy in loads:
        copy.start()

    sx, sy = lax.axis_index("sx"), lax.axis_index("sy")
    rem, div = lax.rem, lax.div
    xl, z, yy, s4 = div(sx, 4), rem(sx, 4), div(sy, 4), rem(sy, 4)
    xh, c = div(s4, 2), rem(s4, 2)
    x = 2 * xh + xl
    j = sx * 4 + s4

    turn = [None, 1 + 2 * c, 2, 3 - 2 * c]
    zs = [z] + [rem(z + turn[d], 4) for d in (1, 2, 3)]
    xt = [x] + [rem(x + turn[d], 4) for d in (1, 2, 3)]
    ys = [yy] + [rem(yy + turn[d], 4) for d in (1, 2, 3)]
    xls, xhs, cs = [rem(v, 2) for v in xt], [div(v, 2) for v in xt], [c, 1 - c]
    zback = [[z] + [rem(z + 4 - turn_, 4) for turn_ in tt] for tt in (
        (1 + 2 * c, 2, 3 - 2 * c), (3 - 2 * c, 2, 1 + 2 * c))]
    xback = [[x] + [rem(x + 4 - turn_, 4) for turn_ in tt] for tt in (
        (1 + 2 * c, 2, 3 - 2 * c), (3 - 2 * c, 2, 1 + 2 * c))]

    def peer(k):
        dz, dx, dc = k % 4, (k // 4) % 4, k // 16
        return xls[dx] * 4 + zs[dz], xhs[dx] * 2 + cs[dc]

    def source(k):
        dz, dx, dc = k % 4, (k // 4) % 4, k // 16
        zz, xx = zback[dc][dz], xback[dc][dx]
        return rem(xx, 2) * 4 + zz, div(xx, 2) * 2 + cs[dc]

    def remote(src, dst, ss, rr, dev):
        return pltpu.make_async_remote_copy(
            src_ref=src, dst_ref=dst, send_sem=ss, recv_sem=rr, device_id=dev, device_id_type=MESH
        )

    sibling = (sx, sy + 1 - 2 * c)

    def bulk(ref, sem):
        return remote(ref, ref, sem, sem, sibling)

    for u in (u0, u1, u2, u3, u4):
        u[0] = jnp.zeros(u.shape[1:], BF16)
        u[17] = jnp.zeros(u.shape[1:], BF16)
        for b in (0, 1, 10, 11):
            u[:, b] = jnp.zeros((18, 16, 256), BF16)
    d0[:, 0] = jnp.zeros((16, 1, 256), F32)
    d0[:, 9] = jnp.zeros((16, 1, 256), F32)

    barrier = pltpu.get_barrier_semaphore()

    for k in range(1, GROUP):
        px, p4 = peer(k)
        pl.semaphore_signal(barrier, inc=1, device_id=(px, yy * 4 + p4), device_id_type=MESH)
    for dy in (1, 2, 3):
        pl.semaphore_signal(barrier, inc=1, device_id=(sx, ys[dy] * 4 + s4), device_id_type=MESH)

    eye = (
        lax.broadcasted_iota(jnp.int32, (256, 256), 0)
        == lax.broadcasted_iota(jnp.int32, (256, 256), 1)
    ).astype(F32).astype(BF16)
    loads[0].wait()
    loads[1].wait()
    for a in range(2):
        for b in range(2):
            nodes = wave[a, 4 * b : 4 * b + 4].reshape(256, 512)
            for h in range(2):
                t[a, b, 256 * h : 256 * h + 256] = lax.dot_general(
                    eye, nodes[:, 256 * h : 256 * h + 256], NT, preferred_element_type=F32
                ).astype(BF16)
            d0[2 * sx + a, 1 + 2 * s4 + b] = jnp.concatenate(
                [pot[a, 4 * b + i : 4 * b + i + 1, :] for i in range(4)], axis=1
            )

    pl.semaphore_wait(barrier, GROUP - 1 + 3)

    xs = pl.ds(1 + 2 * sx, 2)
    bs = pl.ds(2 + 2 * s4, 2)
    own_pot = d0.at[pl.ds(2 * sx, 2), pl.ds(1 + 2 * s4, 2)]

    def cols(i):
        return pl.ds(pl.multiple_of(16 * i, 16), 16)

    def in_copy(k):
        px, p4 = peer(k)
        return remote(
            t.at[:, :, cols(px * 4 + p4)], u0.at[xs, bs], in_s.at[0], in_r.at[k], (px, yy * 4 + p4)
        )

    for k in range(1, GROUP):
        px, p4 = peer(k)
        remote(own_pot, own_pot, pin_s.at[0], pin_r.at[0], (px, yy * 4 + p4)).start()
    for k in range(1, GROUP):
        in_copy(k).start()

    u0[xs, bs] = t[:, :, cols(j)]

    def edge_ends(side):
        far = rem(yy + 3 + 2 * side, 4)
        return ((2, 10) if side == 0 else (9, 1)) + ((sx, far * 4 + s4),)

    def send_on(s, quarter):
        def send(side):
            mine, theirs, dev = edge_ends(side)
            ux = pl.ds(1 + 2 * s, 2)
            remote(u0.at[ux, mine], u0.at[ux, theirs], hal_s.at[side], hal_r.at[side], dev).start()

        @pl.when(jnp.logical_and(quarter == 0, yy > 0))
        def _():
            send(0)

        @pl.when(jnp.logical_and(quarter == 3, yy < 3))
        def _():
            send(1)

    def pot_edge(side):
        mine, theirs, dev = edge_ends(side)
        return remote(
            d0.at[:, mine - 1], d0.at[:, theirs - 1], phal_s.at[side], phal_r.at[side], dev
        )

    bulk(rs.at[0, 1:GROUP], pin_r.at[0]).wait_recv()

    @pl.when(yy > 0)
    def _():
        pot_edge(0).start()

    @pl.when(yy < 3)
    def _():
        pot_edge(1).start()

    send_on(sx, s4)
    for k in range(1, GROUP):
        in_copy(k).wait_recv()
        send_on(*source(k))

    loads[2].wait()
    centre = 0.5 * (high[0] + low[0])
    inv_radius = 1.0 / (0.5 * (high[0] - low[0]))

    def stencil(u, x0, lo, hi):
        n = hi - lo
        rows = 4 * n * 16
        own, edge = [], []
        for dx in (1, 0, 2):
            px = pl.ds(x0 + dx, 4)
            own.append(u[px, lo:hi].reshape(rows, 256))
            nxt = u[px, lo + 1 : hi + 1, :, 0:128].reshape(rows, 128)
            prv = u[px, lo - 1 : hi - 1, :, 128:256].reshape(rows, 128)
            first = lax.broadcasted_iota(jnp.int32, (rows, 128), 1) < 64
            edge.append(jnp.where(first, nxt, prv))
        lhs = jnp.concatenate(own + edge, axis=1)
        acc = jnp.dot(lhs, w_in[...], preferred_element_type=F32)
        return acc.reshape(4, n, 16, 256)

    def apply_step(u, prev, out, lo, hi):
        @pl.loop(0, 4)
        def _(i):
            x0 = 4 * i
            acc = stencil(u, x0, lo, hi)
            px = pl.ds(x0 + 1, 4)
            v = u[px, lo:hi].astype(F32)
            d = (d0[pl.ds(x0, 4), lo - 1 : hi - 1] - centre) * inv_radius
            if prev is None:
                res = acc * (inv_radius / 72.0) + d * v
            else:
                res = acc * (inv_radius / 36.0) + (2.0 * d) * v - prev[px, lo:hi].astype(F32)
            out[px, lo:hi] = res.astype(BF16)

    def outside_zero(out):
        @pl.when(yy == 0)
        def _():
            out[:, 1] = jnp.zeros((18, 16, 256), BF16)

        @pl.when(yy == 3)
        def _():
            out[:, 10] = jnp.zeros((18, 16, 256), BF16)

    apply_step(u0, None, u1, 3, 9)

    def halo_wait(side):
        bulk(u0.at[1:17, 2], hal_r.at[side]).wait_recv()
        pot_edge(side).wait_recv()

    @pl.when(yy < 3)
    def _():
        halo_wait(0)

    @pl.when(yy > 0)
    def _():
        halo_wait(1)

    apply_step(u0, None, u1, 1, 3)
    apply_step(u0, None, u1, 9, 11)
    outside_zero(u1)
    apply_step(u1, u0, u2, 1, 11)
    outside_zero(u2)
    apply_step(u2, u1, u3, 1, 11)
    outside_zero(u3)
    apply_step(u3, u2, u4, 2, 10)

    def layer(side):
        far = rem(yy + 3 + 2 * side, 4)
        mine, theirs, lanes = (2, 10, pl.ds(0, 128)) if side == 0 else (9, 1, pl.ds(128, 128))
        return remote(
            u4.at[pl.ds(1, 16), mine, :, lanes],
            u4.at[pl.ds(1, 16), theirs, :, lanes],
            edge_s.at[side], edge_r.at[side], (sx, far * 4 + s4),
        )

    @pl.when(yy > 0)
    def _():
        layer(0).start()

    @pl.when(yy < 3)
    def _():
        layer(1).start()

    def send_out(src, dst, ss, rr, first):
        for k in range(1, GROUP):
            px, p4 = peer(k)
            remote(
                src.at[pl.ds(first + 2 * px, 2), pl.ds(2 * first + 2 * p4, 2)],
                dst.at[:, :, cols(j)], ss.at[0], rr.at[0], (px, yy * 4 + p4),
            ).start()

    send_out(u4, rf, f_s, f_r, 1)
    rf[:, :, cols(j)] = u4[xs, bs]

    @pl.when(yy < 3)
    def _():
        layer(0).wait_recv()

    @pl.when(yy > 0)
    def _():
        layer(1).wait_recv()

    @pl.loop(0, 4)
    def _(i):
        x0 = 4 * i
        acc = stencil(u4, x0, 2, 10)
        v = u4[pl.ds(x0 + 1, 4), 2:10].astype(F32)
        res = acc * (1.0 / 72.0) + d0[pl.ds(x0, 4), 1:9] * v
        img[pl.ds(x0, 4)] = res.astype(BF16)

    send_out(img, ri, i_s, i_r, 0)
    ri[:, :, cols(j)] = img[pl.ds(2 * sx, 2), pl.ds(2 * s4, 2)]

    def core_copy(n):
        return remote(
            part.at[n, :, 1 - c], other.at[n], core_s.at[n], core_r.at[n], sibling
        )

    def gram(n, right):
        whole = jnp.concatenate([rf[a, b] for a in range(2) for b in range(2)], axis=1)
        with_ = jnp.concatenate([right[a, b] for a in range(2) for b in range(2)], axis=1)
        for r in range(4):
            g = lax.dot_general(
                whole[128 * r : 128 * r + 128], with_, NT, preferred_element_type=F32
            ).reshape(2, 2, 2, 16, 512)
            gm[2 * r : 2 * r + 2] = g
            part[n, 2 * r : 2 * r + 2] = g.astype(BF16)
        core_copy(n).start()

    def rs_copy(n, k):
        dz, dx, dy = k % 4, (k // 4) % 4, k // 16
        m, h, q = ys[dy] * 2 + xhs[dx], xls[dx], zs[dz]
        return remote(
            half.at[n, m, h, :, pl.ds(pl.multiple_of(128 * q, 128), 128)],
            rs.at[n, k], rs_s.at[n], rs_r.at[n], (h * 4 + q, m * 2 + c),
        )

    def scatter(n):
        core_copy(n).wait_recv()
        half[n] = (gm[:, c] + other[n].astype(F32)).astype(BF16)

        for k in range(1, 64):
            rs_copy(n, k).start()

        rs[n, 0] = half[n, 2 * yy + xh, xl, :, pl.ds(pl.multiple_of(128 * z, 128), 128)]

    def collect(n):
        bulk(rs.at[n, 1:64], rs_r.at[n]).wait_recv()
        ob[sx, n] = jnp.sum(rs[n].astype(F32), axis=0) * (1.0 / 131072.0)

    bulk(t.at[:, :, 0:496], f_r.at[0]).wait_recv()
    gram(0, rf)
    scatter(0)

    bulk(t.at[:, :, 0:496], i_r.at[0]).wait_recv()
    gram(1, ri)
    scatter(1)
    collect(0)
    collect(1)

    for k in range(1, 8):
        far = rem(sx + k, 8)
        remote(ob.at[sx], ob.at[sx], ag_s.at[0], ag_r.at[0], (far, sy)).start()

    for sem in (in_s, f_s, i_s):
        bulk(t.at[:, :, 0:496], sem.at[0]).wait_send()
    bulk(rs.at[0, 1:GROUP], pin_s.at[0]).wait_send()

    def sent(side):
        bulk(u0.at[1:17, 2], hal_s.at[side]).wait_send()
        pot_edge(side).wait_send()
        layer(side).wait_send()

    @pl.when(yy > 0)
    def _():
        sent(0)

    @pl.when(yy < 3)
    def _():
        sent(1)

    for n in range(2):
        core_copy(n).wait_send()
        bulk(rs.at[n, 1:64], rs_s.at[n]).wait_send()
    bulk(ob.at[0:7], ag_s.at[0]).wait_send()
    bulk(ob.at[0:7], ag_r.at[0]).wait_recv()
    for s in range(8):
        rows, lanes = pl.ds(16 * (s // 4), 16), pl.ds(128 * (s % 4), 128)
        margin[rows, lanes] = ob[s, 0]
        projected[rows, lanes] = ob[s, 1]


def on_device(wave, potential, lower_cut, upper_edge):
    dma = pltpu.SemaphoreType.DMA
    field = pltpu.VMEM((18, 12, 16, 256), BF16)
    block = pltpu.VMEM((2, 2, 512, 256), BF16)
    vmem = pl.BlockSpec(memory_space=pltpu.VMEM)
    hbm = pl.BlockSpec(memory_space=pl.ANY)
    smem = pl.BlockSpec(memory_space=pltpu.SMEM)
    weights = jnp.asarray(stencil_matrix(), BF16)
    return pl.pallas_call(
        kernel,
        out_shape=[jax.ShapeDtypeStruct((32, 512), F32)] * 2,
        in_specs=[hbm, hbm, smem, smem, hbm],
        out_specs=[vmem, vmem],
        scratch_shapes=[
            pltpu.VMEM(wave.shape, BF16),
            pltpu.VMEM(potential.shape, F32),
            pltpu.VMEM(weights.shape, BF16),
            block,
            field, field, field, field, field,
            pltpu.VMEM((16, 8, 16, 256), BF16),
            pltpu.VMEM((16, 10, 1, 256), F32),
            block, block,
            pltpu.VMEM((8, 2, 2, 16, 512), F32),
            pltpu.VMEM((2, 8, 2, 2, 16, 512), BF16),
            pltpu.VMEM((2, 8, 2, 16, 512), BF16),
            pltpu.VMEM((2, 8, 2, 16, 512), BF16),
            pltpu.VMEM((2, 64, 16, 128), BF16),
            pltpu.VMEM((8, 2, 16, 128), F32),
            dma((3,)), dma((1,)), dma((32,)), dma((1,)), dma((1,)),
            dma((2,)), dma((2,)), dma((2,)), dma((2,)),
            dma((2,)), dma((2,)),
            dma((1,)), dma((1,)), dma((1,)), dma((1,)),
            dma((2,)), dma((2,)), dma((2,)), dma((2,)),
            dma((1,)), dma((1,)),
        ],
        compiler_params=pltpu.CompilerParams(
            collective_id=0, has_side_effects=True, vmem_limit_bytes=127 << 19
        ),
    )(wave, potential, lower_cut, upper_edge, weights)


def solution(mesh):
    return jax.shard_map(
        on_device,
        mesh=mesh,
        in_specs=(P("sx", "sy", None, None), P("sx", "sy", None), P(), P()),
        out_specs=(P("sy", None), P("sy", None)),
        check_vma=False,
    )
```

```python
import functools

import jax
import jax.numpy as jnp
import numpy as np
from jax import lax
from jax.experimental import pallas as pl
from jax.experimental.pallas import tpu as pltpu
from jax.sharding import PartitionSpec as P

MESH = pl.DeviceIdType.MESH
F32, BF16 = jnp.float32, jnp.bfloat16
GROUP = 32
FIRST = (2, 8)
PLANE = (10, 6, 14, 9, 11, 5, 7, 13, 15, 1, 3, 4, 12)
OTHER = (26, 22, 30, 25, 27, 18, 24, 21, 23, 29, 31, 17, 19, 20, 28, 16)
NT = (((1,), (1,)), ((), ()))


def stencil_matrix():
    my, ky = np.zeros((4, 6)), np.zeros((4, 6))
    for i in range(4):
        my[i, i : i + 3] = 1, 4, 1
        ky[i, i : i + 3] = -1, 2, -1
    mz, kz = np.zeros((64, 64)), np.zeros((64, 64))
    for i in range(64):
        for j in range(max(i - 1, 0), min(i + 2, 64)):
            mz[i, j] = 4 if i == j else 1
            kz[i, j] = 2 if i == j else -1
    m = np.einsum("ij,kl->jlik", my, mz).reshape(6, 64, 256)
    g = np.einsum("ij,kl->jlik", ky, mz) + np.einsum("ij,kl->jlik", my, kz)
    g = g.reshape(6, 64, 256)
    p, q = 2 * m + 4 * g, g - m
    own = lambda t: t[1:5].reshape(256, 256)
    edge = lambda t: np.concatenate([t[5], t[0]], axis=0)
    return np.concatenate([own(p), own(q), edge(p), edge(q)], axis=0)


def kernel(
    wave_hbm, pot_hbm, low, high, w_hbm, margin, projected,
    wave, pot, w_in, t, u0, u1, u2, u3, u4, co, ce, d0, rf, rco, rce, loc, ri, gm, part, other, half, rs, ob,
    load, in_s, in_r, pin_s, pin_r, hal_s, hal_r, phal_s, phal_r, edge_s, edge_r,
    f_s, f_r, i_s, i_r, core_s, core_r, rs_s, rs_r, ag_s, ag_r, plane, chip,
):
    loads = [
        pltpu.make_async_copy(src, dst, load.at[i])
        for i, (src, dst) in enumerate([(wave_hbm, wave), (pot_hbm, pot), (w_hbm, w_in)])
    ]
    for copy in loads:
        copy.start()

    sx, sy = lax.axis_index("sx"), lax.axis_index("sy")
    rem, div = lax.rem, lax.div
    xl, z, yy, s4 = div(sx, 4), rem(sx, 4), div(sy, 4), rem(sy, 4)
    xh, c = div(s4, 2), rem(s4, 2)
    x = 2 * xh + xl
    j = sx * 4 + s4

    turn = [None, 1 + 2 * c, 2, 3 - 2 * c]
    zs = [z] + [rem(z + turn[d], 4) for d in (1, 2, 3)]
    xt = [x] + [rem(x + turn[d], 4) for d in (1, 2, 3)]
    ys = [yy] + [rem(yy + turn[d], 4) for d in (1, 2, 3)]
    xls, xhs, cs = [rem(v, 2) for v in xt], [div(v, 2) for v in xt], [c, 1 - c]
    zback = [[z] + [rem(z + 4 - turn_, 4) for turn_ in tt] for tt in (
        (1 + 2 * c, 2, 3 - 2 * c), (3 - 2 * c, 2, 1 + 2 * c))]
    xback = [[x] + [rem(x + 4 - turn_, 4) for turn_ in tt] for tt in (
        (1 + 2 * c, 2, 3 - 2 * c), (3 - 2 * c, 2, 1 + 2 * c))]

    def peer(k):
        dz, dx, dc = k % 4, (k // 4) % 4, k // 16
        return xls[dx] * 4 + zs[dz], xhs[dx] * 2 + cs[dc]

    def source(k):
        dz, dx, dc = k % 4, (k // 4) % 4, k // 16
        zz, xx = zback[dc][dz], xback[dc][dx]
        return rem(xx, 2) * 4 + zz, div(xx, 2) * 2 + cs[dc]

    def remote(src, dst, ss, rr, dev):
        return pltpu.make_async_remote_copy(
            src_ref=src, dst_ref=dst, send_sem=ss, recv_sem=rr, device_id=dev, device_id_type=MESH
        )

    sibling = (sx, sy + 1 - 2 * c)

    def bulk(ref, sem):
        return remote(ref, ref, sem, sem, sibling)

    for u in (u0, u1, u2, u3, u4):
        u[0] = jnp.zeros(u.shape[1:], BF16)
        u[17] = jnp.zeros(u.shape[1:], BF16)
        for b in (0, 1, 10, 11):
            u[:, b] = jnp.zeros((18, 16, 256), BF16)
    d0[:, 0] = jnp.zeros((16, 1, 256), F32)
    d0[:, 9] = jnp.zeros((16, 1, 256), F32)

    barrier = pltpu.get_barrier_semaphore()
    direct = [(px, yy * 4 + p4) for px, p4 in (peer(k) for k in (1, 2, 3, 4, 8, 12, 16))]
    direct += [(sx, ys[dy] * 4 + s4) for dy in (1, 2, 3)]
    for dev in direct:
        pl.semaphore_signal(barrier, inc=1, device_id=dev, device_id_type=MESH)

    eye = (
        lax.broadcasted_iota(jnp.int32, (256, 256), 0)
        == lax.broadcasted_iota(jnp.int32, (256, 256), 1)
    ).astype(F32).astype(BF16)
    loads[0].wait()
    loads[1].wait()
    for a in range(2):
        for b in range(2):
            nodes = wave[a, 4 * b : 4 * b + 4].reshape(256, 512)
            for h in range(2):
                turned = lax.dot_general(
                    eye, nodes[:, 256 * h : 256 * h + 256], NT, preferred_element_type=F32
                )
                t[16 * h : 16 * h + 16, a, b] = turned.astype(BF16).reshape(16, 16, 256)
            d0[2 * sx + a, 1 + 2 * s4 + b] = jnp.concatenate(
                [pot[a, 4 * b + i : 4 * b + i + 1, :] for i in range(4)], axis=1
            )

    pl.semaphore_wait(barrier, len(direct))

    xs = pl.ds(1 + 2 * sx, 2)
    bs = pl.ds(2 + 2 * s4, 2)
    own_pot = d0.at[pl.ds(2 * sx, 2), pl.ds(1 + 2 * s4, 2)]

    def in_copy(k):
        px, p4 = peer(k)
        return remote(
            t.at[px * 4 + p4], u0.at[xs, bs], in_s.at[0], in_r.at[k], (px, yy * 4 + p4)
        )

    def send_in(ks):
        for k in ks:
            px, p4 = peer(k)
            remote(own_pot, own_pot, pin_s.at[0], pin_r.at[0], (px, yy * 4 + p4)).start()
            in_copy(k).start()

    for k in (1, 2, 3):
        px, p4 = peer(k)
        pl.semaphore_signal(plane, inc=1, device_id=(px, yy * 4 + p4), device_id_type=MESH)
    send_in(FIRST)
    pl.semaphore_wait(plane, 3)
    pl.semaphore_signal(chip, inc=1, device_id=sibling, device_id_type=MESH)
    send_in(PLANE)
    pl.semaphore_wait(chip, 1)
    send_in(OTHER)

    u0[xs, bs] = t[j]

    def edge_ends(side):
        far = rem(yy + 3 + 2 * side, 4)
        return ((2, 10) if side == 0 else (9, 1)) + ((sx, far * 4 + s4),)

    def send_on(s, quarter):
        def send(side):
            mine, theirs, dev = edge_ends(side)
            ux = pl.ds(1 + 2 * s, 2)
            remote(u0.at[ux, mine], u0.at[ux, theirs], hal_s.at[side], hal_r.at[side], dev).start()

        @pl.when(jnp.logical_and(quarter == 0, yy > 0))
        def _():
            send(0)

        @pl.when(jnp.logical_and(quarter == 3, yy < 3))
        def _():
            send(1)

    def pot_edge(side):
        mine, theirs, dev = edge_ends(side)
        return remote(
            d0.at[:, mine - 1], d0.at[:, theirs - 1], phal_s.at[side], phal_r.at[side], dev
        )

    bulk(rs.at[0, 1:GROUP], pin_r.at[0]).wait_recv()

    @pl.when(yy > 0)
    def _():
        pot_edge(0).start()

    @pl.when(yy < 3)
    def _():
        pot_edge(1).start()

    send_on(sx, s4)
    for k in (*FIRST, *PLANE, *OTHER):
        in_copy(k).wait_recv()
        send_on(*source(k))

    loads[2].wait()
    centre = 0.5 * (high[0] + low[0])
    inv_radius = 1.0 / (0.5 * (high[0] - low[0]))

    def edge_slab(nxt, prv):
        return jnp.where(lax.broadcasted_iota(jnp.int32, nxt.shape, len(nxt.shape) - 1) < 64, nxt, prv)

    def stencil(u, x0, lo, hi):
        n = hi - lo
        rows = 4 * n * 16
        mid = u[pl.ds(x0 + 1, 4), lo - 1 : hi + 1]
        beside = u[pl.ds(x0, 4), lo - 1 : hi + 1] + u[pl.ds(x0 + 2, 4), lo - 1 : hi + 1]
        slabs = [v[:, 1 : n + 1].reshape(rows, 256) for v in (mid, beside)]
        slabs += [
            edge_slab(v[:, 2:, :, 0:128], v[:, :n, :, 128:256]).reshape(rows, 128)
            for v in (mid, beside)
        ]
        acc = jnp.dot(jnp.concatenate(slabs, axis=1), w_in[...], preferred_element_type=F32)
        return acc.reshape(4, n, 16, 256)

    def apply_chunk(u, prev, out, x0, lo, hi):
        acc = stencil(u, x0, lo, hi)
        px = pl.ds(x0 + 1, 4)
        v = u[px, lo:hi].astype(F32)
        d = (d0[pl.ds(x0, 4), lo - 1 : hi - 1] - centre) * inv_radius
        if prev is None:
            res = acc * (inv_radius / 72.0) + d * v
        else:
            res = acc * (inv_radius / 36.0) + (2.0 * d) * v - prev[px, lo:hi].astype(F32)
        out[px, lo:hi] = res.astype(BF16)

    def apply_step(u, prev, out, lo, hi):
        @pl.loop(0, 4, unroll=4)
        def _(i):
            apply_chunk(u, prev, out, 4 * i, lo, hi)

    def outside_zero(out):
        @pl.when(yy == 0)
        def _():
            out[:, 1] = jnp.zeros((18, 16, 256), BF16)

        @pl.when(yy == 3)
        def _():
            out[:, 10] = jnp.zeros((18, 16, 256), BF16)

    apply_step(u0, None, u1, 3, 9)

    def halo_wait(side):
        bulk(u0.at[1:17, 2], hal_r.at[side]).wait_recv()
        pot_edge(side).wait_recv()

    @pl.when(yy < 3)
    def _():
        halo_wait(0)

    @pl.when(yy > 0)
    def _():
        halo_wait(1)

    apply_step(u0, None, u1, 1, 3)
    apply_step(u0, None, u1, 9, 11)
    outside_zero(u1)
    apply_step(u1, u0, u2, 1, 11)
    outside_zero(u2)
    apply_step(u2, u1, u3, 1, 11)
    outside_zero(u3)
    apply_step(u3, u2, u4, 2, 10)

    def layer(side):
        far = rem(yy + 3 + 2 * side, 4)
        mine, theirs, lanes = (2, 10, pl.ds(0, 128)) if side == 0 else (9, 1, pl.ds(128, 128))
        return remote(
            u4.at[pl.ds(1, 16), mine, :, lanes],
            u4.at[pl.ds(1, 16), theirs, :, lanes],
            edge_s.at[side], edge_r.at[side], (sx, far * 4 + s4),
        )

    @pl.when(yy > 0)
    def _():
        layer(0).start()

    @pl.when(yy < 3)
    def _():
        layer(1).start()

    def send_out(src, dst, ss, rr, first):
        for k in (*OTHER, *PLANE, *FIRST):
            px, p4 = peer(k)
            remote(
                src.at[pl.ds(first + 2 * px, 2), pl.ds(2 * first + 2 * p4, 2)],
                dst.at[j], ss.at[0], rr.at[0], (px, yy * 4 + p4),
            ).start()

    send_out(u4, rf, f_s, f_r, 1)
    rf[j] = u4[xs, bs]

    @pl.when(yy < 3)
    def _():
        layer(0).wait_recv()

    @pl.when(yy > 0)
    def _():
        layer(1).wait_recv()

    zero = jnp.zeros((), BF16)

    @pl.loop(0, 2)
    def _(i):
        own, slab_p, slab_q, even_p, even_q = [], [], [], [], []
        first = lax.broadcasted_iota(jnp.int32, (8, 16, 128), 2) < 64
        last = lax.broadcasted_iota(jnp.int32, (8, 16, 128), 0) % 2 == 1
        for m in range(4):
            before, here, after = (u4.at[8 * i + 2 * m + n] for n in (1, 2, 3))
            own.append(after[2:10].reshape(128, 256))
            nxt = [u[3:11, :, 0:128] for u in (before, here, after)]
            slab_p.append(jnp.where(first & last, nxt[1], zero).reshape(128, 128))
            far = nxt[2] + jnp.where(last, nxt[0], zero)
            slab_q.append(jnp.where(first, far, after[1:9, :, 128:256]).reshape(128, 128))
            for b in (4, 6, 8, 10):
                even_p.append(jnp.where(first[0], before[b, :, 0:128], zero))
                even_q.append(jnp.where(first[0], here[b, :, 0:128], zero))
        join = lambda parts: jnp.concatenate(parts, axis=0)
        lhs = jnp.concatenate([join(own), join(slab_p), join(slab_q)], axis=1)
        acc = jnp.dot(lhs, w_in[256:768], preferred_element_type=F32) * (2.0 / 72.0)
        co[pl.ds(4 * i, 4)] = acc.astype(BF16).reshape(4, 8, 16, 256)
        lhs = jnp.concatenate([join(even_p), join(even_q)], axis=1)
        acc = jnp.dot(lhs, w_in[512:768, 128:256], preferred_element_type=F32) * (2.0 / 72.0)
        ce[pl.ds(4 * i, 4)] = acc.astype(BF16).reshape(4, 4, 16, 128)

    for k in (*OTHER, *PLANE, *FIRST):
        px, p4 = peer(k)
        dev = (px, yy * 4 + p4)
        remote(co.at[px, pl.ds(2 * p4, 2)], rco.at[j], i_s.at[0], i_r.at[0], dev).start()
        remote(ce.at[px, p4], rce.at[j], i_s.at[1], i_r.at[1], dev).start()
    rco[j] = co[sx, pl.ds(2 * s4, 2)]
    rce[j] = ce[sx, s4]

    def core_copy(n):
        return remote(
            part.at[n, :, 1 - c], other.at[n], core_s.at[n], core_r.at[n], sibling
        )

    units = [(a, b) for a in range(2) for b in range(2)]

    def flat(ref):
        return ref.reshape(512, ref.shape[-1])

    def gram(n, left, right):
        for r in range(4):
            g = lax.dot_general(
                left[128 * r : 128 * r + 128], right, NT, preferred_element_type=F32
            ).reshape(2, 2, 2, 16, 512)
            gm[2 * r : 2 * r + 2] = g
            part[n, 2 * r : 2 * r + 2] = g.astype(BF16)
        core_copy(n).start()

    def local_image():
        first = lax.broadcasted_iota(jnp.int32, (512, 128), 1) < 64
        for a, b in units:
            slabs = [flat(rf[:, n, b]) for n in (a, 1 - a)]
            for n in (a, 1 - a):
                if b == 0:
                    slabs.append(jnp.where(first, flat(rf[:, n, 1, :, 0:128]), zero))
                else:
                    slabs.append(jnp.where(first, zero, flat(rf[:, n, 0, :, 128:256])))
            acc = jnp.dot(jnp.concatenate(slabs, axis=1), w_in[...], preferred_element_type=F32)
            here = d0[2 * sx + a, 1 + 2 * s4 + b] * flat(rf[:, a, b]).astype(F32)
            loc[a, b] = acc * (1.0 / 72.0) + here

    def whole_image():
        for a, b in units:
            full = loc[a, b]
            if a == 1:
                full += flat(rco[:, b]).astype(F32)
            elif b == 1:
                far = flat(rce[...]).astype(F32)
                full += jnp.concatenate([jnp.zeros((512, 128), F32), far], axis=1)
            ri[a, b] = full.astype(BF16)

    def rs_copy(n, k):
        dz, dx, dy = k % 4, (k // 4) % 4, k // 16
        m, h, q = ys[dy] * 2 + xhs[dx], xls[dx], zs[dz]
        return remote(
            half.at[n, m, h, :, pl.ds(pl.multiple_of(128 * q, 128), 128)],
            rs.at[n, k], rs_s.at[n], rs_r.at[n], (h * 4 + q, m * 2 + c),
        )

    def scatter(n):
        core_copy(n).wait_recv()
        half[n] = (gm[:, c] + other[n].astype(F32)).astype(BF16)

        for k in range(1, 64):
            rs_copy(n, k).start()

        rs[n, 0] = half[n, 2 * yy + xh, xl, :, pl.ds(pl.multiple_of(128 * z, 128), 128)]

    def collect(n):
        bulk(rs.at[n, 1:64], rs_r.at[n]).wait_recv()
        ob[sx, n] = jnp.sum(rs[n].astype(F32), axis=0) * ((1.0 - 0.5 * n) / 131072.0)

    bulk(t.at[1:GROUP], f_r.at[0]).wait_recv()
    field_rows = jnp.concatenate([flat(rf[:, a, b]) for a, b in units], axis=1)
    gram(0, field_rows, field_rows)
    local_image()
    scatter(0)

    bulk(t.at[1:GROUP, 0], i_r.at[0]).wait_recv()
    bulk(rs.at[0, 1:GROUP], i_r.at[1]).wait_recv()
    whole_image()
    field_rows = [flat(rf[:, a, b]) for a, b in units]
    image_rows = [ri[a, b] for a, b in units]
    gram(
        1,
        jnp.concatenate(field_rows + image_rows, axis=1),
        jnp.concatenate(image_rows + field_rows, axis=1),
    )
    scatter(1)
    collect(0)
    collect(1)

    for k in range(1, 8):
        far = rem(sx + k, 8)
        remote(ob.at[sx], ob.at[sx], ag_s.at[0], ag_r.at[0], (far, sy)).start()

    for sem in (in_s, f_s):
        bulk(t.at[1:GROUP], sem.at[0]).wait_send()
    bulk(t.at[1:GROUP, 0], i_s.at[0]).wait_send()
    bulk(rs.at[0, 1:GROUP], i_s.at[1]).wait_send()
    bulk(rs.at[0, 1:GROUP], pin_s.at[0]).wait_send()

    def sent(side):
        bulk(u0.at[1:17, 2], hal_s.at[side]).wait_send()
        pot_edge(side).wait_send()
        layer(side).wait_send()

    @pl.when(yy > 0)
    def _():
        sent(0)

    @pl.when(yy < 3)
    def _():
        sent(1)

    for n in range(2):
        core_copy(n).wait_send()
        bulk(rs.at[n, 1:64], rs_s.at[n]).wait_send()
    bulk(ob.at[0:7], ag_s.at[0]).wait_send()
    bulk(ob.at[0:7], ag_r.at[0]).wait_recv()
    for s in range(8):
        rows, lanes = pl.ds(16 * (s // 4), 16), pl.ds(128 * (s % 4), 128)
        margin[rows, lanes] = ob[s, 0]
        projected[rows, lanes] = ob[s, 1]


def on_device(wave, potential, lower_cut, upper_edge):
    dma = pltpu.SemaphoreType.DMA
    field = pltpu.VMEM((18, 12, 16, 256), BF16)
    block = pltpu.VMEM((GROUP, 2, 2, 16, 256), BF16)
    vmem = pl.BlockSpec(memory_space=pltpu.VMEM)
    hbm = pl.BlockSpec(memory_space=pl.ANY)
    smem = pl.BlockSpec(memory_space=pltpu.SMEM)
    weights = jnp.asarray(stencil_matrix(), BF16)
    return pl.pallas_call(
        kernel,
        out_shape=[jax.ShapeDtypeStruct((32, 512), F32)] * 2,
        in_specs=[hbm, hbm, smem, smem, hbm],
        out_specs=[vmem, vmem],
        scratch_shapes=[
            pltpu.VMEM(wave.shape, BF16),
            pltpu.VMEM(potential.shape, F32),
            pltpu.VMEM(weights.shape, BF16),
            block,
            field, field, field, field, field,
            pltpu.VMEM((8, 8, 16, 256), BF16),
            pltpu.VMEM((8, 4, 16, 128), BF16),
            pltpu.VMEM((16, 10, 1, 256), F32),
            block,
            pltpu.VMEM((GROUP, 2, 16, 256), BF16),
            pltpu.VMEM((GROUP, 16, 128), BF16),
            pltpu.VMEM((2, 2, 512, 256), F32),
            pltpu.VMEM((2, 2, 512, 256), BF16),
            pltpu.VMEM((8, 2, 2, 16, 512), F32),
            pltpu.VMEM((2, 8, 2, 2, 16, 512), BF16),
            pltpu.VMEM((2, 8, 2, 16, 512), BF16),
            pltpu.VMEM((2, 8, 2, 16, 512), BF16),
            pltpu.VMEM((2, 64, 16, 128), BF16),
            pltpu.VMEM((8, 2, 16, 128), F32),
            dma((3,)), dma((1,)), dma((32,)), dma((1,)), dma((1,)),
            dma((2,)), dma((2,)), dma((2,)), dma((2,)),
            dma((2,)), dma((2,)),
            dma((1,)), dma((1,)), dma((2,)), dma((2,)),
            dma((2,)), dma((2,)), dma((2,)), dma((2,)),
            dma((1,)), dma((1,)),
            pltpu.SemaphoreType.REGULAR, pltpu.SemaphoreType.REGULAR,
        ],
        compiler_params=pltpu.CompilerParams(
            collective_id=0, has_side_effects=True, vmem_limit_bytes=127 << 19
        ),
    )(wave, potential, lower_cut, upper_edge, weights)


def solution(mesh):
    return jax.shard_map(
        on_device,
        mesh=mesh,
        in_specs=(P("sx", "sy", None, None), P("sx", "sy", None), P(), P()),
        out_specs=(P("sy", None), P("sy", None)),
        check_vma=False,
    )
```

```python
import functools

import jax
import jax.numpy as jnp
import numpy as np
from jax import lax
from jax.experimental import pallas as pl
from jax.experimental.pallas import tpu as pltpu
from jax.sharding import PartitionSpec as P

MESH = pl.DeviceIdType.MESH
F32, BF16 = jnp.float32, jnp.bfloat16
GROUP = 32
FIRST = (2, 8, 1, 3, 4, 12)
PLANE = (10, 6, 14, 9, 11, 5, 7, 13, 15)
OTHER = (26, 22, 30, 25, 27, 18, 24, 21, 23, 29, 31, 17, 19, 20, 28, 16)
NT = (((1,), (1,)), ((), ()))


def stencil_matrix():
    my, ky = np.zeros((4, 6)), np.zeros((4, 6))
    for i in range(4):
        my[i, i : i + 3] = 1, 4, 1
        ky[i, i : i + 3] = -1, 2, -1
    mz, kz = np.zeros((64, 64)), np.zeros((64, 64))
    for i in range(64):
        for j in range(max(i - 1, 0), min(i + 2, 64)):
            mz[i, j] = 4 if i == j else 1
            kz[i, j] = 2 if i == j else -1
    m = np.einsum("ij,kl->jlik", my, mz).reshape(6, 64, 256)
    g = np.einsum("ij,kl->jlik", ky, mz) + np.einsum("ij,kl->jlik", my, kz)
    g = g.reshape(6, 64, 256)
    p, q = 2 * m + 4 * g, g - m
    own = lambda t: t[1:5].reshape(256, 256)
    edge = lambda t: np.concatenate([t[5], t[0]], axis=0)
    return np.concatenate([own(p), own(q), edge(p), edge(q)], axis=0)


def kernel(
    wave_hbm, pot_hbm, low, high, w_hbm, margin, projected,
    wave, pot, w_in, t, u0, u1, u2, u3, u4, co, ce, d0, rf, rco, rce, ri, gm, part, other, half, ysum, plane_part, rs, ob,
    load, in_s, in_r, pin_s, pin_r, hal_s, hal_r, phal_s, phal_r, edge_s, edge_r,
    f_s, f_r, i_s, i_r, core_s, core_r, y_s, y_r, rs_s, rs_r, ag_s, ag_r, plane, chip,
):
    loads = [
        pltpu.make_async_copy(src, dst, load.at[i])
        for i, (src, dst) in enumerate([(wave_hbm, wave), (pot_hbm, pot), (w_hbm, w_in)])
    ]
    for copy in loads:
        copy.start()

    sx, sy = lax.axis_index("sx"), lax.axis_index("sy")
    rem, div = lax.rem, lax.div
    xl, z, yy, s4 = div(sx, 4), rem(sx, 4), div(sy, 4), rem(sy, 4)
    xh, c = div(s4, 2), rem(s4, 2)
    x = 2 * xh + xl
    j = sx * 4 + s4

    turn = [None, 1 + 2 * c, 2, 3 - 2 * c]
    zs = [z] + [rem(z + turn[d], 4) for d in (1, 2, 3)]
    xt = [x] + [rem(x + turn[d], 4) for d in (1, 2, 3)]
    ys = [yy] + [rem(yy + turn[d], 4) for d in (1, 2, 3)]
    xls, xhs, cs = [rem(v, 2) for v in xt], [div(v, 2) for v in xt], [c, 1 - c]
    def peer(k):
        dz, dx, dc = k % 4, (k // 4) % 4, k // 16
        return xls[dx] * 4 + zs[dz], xhs[dx] * 2 + cs[dc]

    def remote(src, dst, ss, rr, dev):
        return pltpu.make_async_remote_copy(
            src_ref=src, dst_ref=dst, send_sem=ss, recv_sem=rr, device_id=dev, device_id_type=MESH
        )

    sibling = (sx, sy + 1 - 2 * c)

    def bulk(ref, sem):
        return remote(ref, ref, sem, sem, sibling)

    for u in (u0, u1, u2, u3, u4):
        u[0] = jnp.zeros(u.shape[1:], BF16)
        u[17] = jnp.zeros(u.shape[1:], BF16)
        for b in (0, 1, 10, 11):
            u[:, b] = jnp.zeros((18, 16, 256), BF16)
    d0[:, 0] = jnp.zeros((16, 1, 256), F32)
    d0[:, 9] = jnp.zeros((16, 1, 256), F32)

    barrier = pltpu.get_barrier_semaphore()
    direct = [(px, yy * 4 + p4) for px, p4 in (peer(k) for k in (1, 2, 3, 4, 8, 12, 16))]
    direct += [(sx, ys[dy] * 4 + s4) for dy in (1, 2, 3)]
    for dev in direct:
        pl.semaphore_signal(barrier, inc=1, device_id=dev, device_id_type=MESH)

    eye = (
        lax.broadcasted_iota(jnp.int32, (256, 256), 0)
        == lax.broadcasted_iota(jnp.int32, (256, 256), 1)
    ).astype(F32).astype(BF16)
    loads[0].wait()
    loads[1].wait()
    for a in range(2):
        for b in range(2):
            nodes = wave[a, 4 * b : 4 * b + 4].reshape(256, 512)
            for h in range(2):
                turned = lax.dot_general(
                    eye, nodes[:, 256 * h : 256 * h + 256], NT, preferred_element_type=F32
                )
                t[16 * h : 16 * h + 16, a, b] = turned.astype(BF16).reshape(16, 16, 256)
            d0[2 * sx + a, 1 + 2 * s4 + b] = jnp.concatenate(
                [pot[a, 4 * b + i : 4 * b + i + 1, :] for i in range(4)], axis=1
            )

    pl.semaphore_wait(barrier, len(direct))

    xs = pl.ds(1 + 2 * sx, 2)
    bs = pl.ds(2 + 2 * s4, 2)
    own_pot = d0.at[pl.ds(2 * sx, 2), pl.ds(1 + 2 * s4, 2)]

    def in_copy(k):
        px, p4 = peer(k)
        return remote(
            t.at[px * 4 + p4], u0.at[xs, bs], in_s.at[0], in_r.at[j], (px, yy * 4 + p4)
        )

    def send_in(ks):
        for k in ks:
            in_copy(k).start()

    def send_pot(strip, stage, devs):
        for dev in devs:
            remote(strip, strip, pin_s.at[stage], pin_r.at[stage], dev).start()

    along_z, along_x = direct[0:3], direct[3:6]
    for dev in along_z:
        pl.semaphore_signal(plane, inc=1, device_id=dev, device_id_type=MESH)
    send_pot(own_pot, 0, along_z)
    send_in(FIRST)
    pl.semaphore_wait(plane, 3)
    pl.semaphore_signal(chip, inc=1, device_id=sibling, device_id_type=MESH)
    bulk(rs.at[0, 0:3], pin_r.at[0]).wait_recv()
    send_pot(d0.at[pl.ds(8 * xl, 8), pl.ds(1 + 2 * s4, 2)], 1, along_x)
    send_in(PLANE)
    pl.semaphore_wait(chip, 1)
    send_in(OTHER)
    bulk(rs.at[0, 0:12], pin_r.at[1]).wait_recv()
    for q in (c, 2 + c):
        send_pot(d0.at[:, pl.ds(1 + 2 * q, 2)], 2, [sibling])

    u0[xs, bs] = t[j]

    def edge_ends(side):
        far = rem(yy + 3 + 2 * side, 4)
        return ((2, 10) if side == 0 else (9, 1)) + ((sx, far * 4 + s4),)

    def send_on(s, quarter):
        side = quarter // 3
        mine, theirs, dev = edge_ends(side)
        ux = pl.ds(1 + 2 * s, 2)

        @pl.when(yy > 0 if side == 0 else yy < 3)
        def _():
            remote(u0.at[ux, mine], u0.at[ux, theirs], hal_s.at[side], hal_r.at[side], dev).start()

    def pot_edge(side):
        mine, theirs, dev = edge_ends(side)
        return remote(
            d0.at[:, mine - 1], d0.at[:, theirs - 1], phal_s.at[side], phal_r.at[side], dev
        )

    bulk(rs.at[0, 0:16], pin_r.at[2]).wait_recv()

    @pl.when(yy > 0)
    def _():
        pot_edge(0).start()

    @pl.when(yy < 3)
    def _():
        pot_edge(1).start()

    def arrived(i):
        @pl.when(j != i)
        def _():
            bulk(u0.at[xs, bs], in_r.at[i]).wait_recv()

    for s in range(8):
        for quarter in (0, 3):
            arrived(4 * s + quarter)
            send_on(s, quarter)
    for s in range(8):
        for quarter in (1, 2):
            arrived(4 * s + quarter)

    loads[2].wait()
    centre = 0.5 * (high[0] + low[0])
    inv_radius = 1.0 / (0.5 * (high[0] - low[0]))

    def edge_slab(nxt, prv):
        return jnp.where(lax.broadcasted_iota(jnp.int32, nxt.shape, len(nxt.shape) - 1) < 64, nxt, prv)

    def stencil(u, x0, lo, hi):
        n = hi - lo
        rows = 4 * n * 16
        mid = u[pl.ds(x0 + 1, 4), lo - 1 : hi + 1]
        beside = u[pl.ds(x0, 4), lo - 1 : hi + 1] + u[pl.ds(x0 + 2, 4), lo - 1 : hi + 1]
        slabs = [v[:, 1 : n + 1].reshape(rows, 256) for v in (mid, beside)]
        slabs += [
            edge_slab(v[:, 2:, :, 0:128], v[:, :n, :, 128:256]).reshape(rows, 128)
            for v in (mid, beside)
        ]
        acc = jnp.dot(jnp.concatenate(slabs, axis=1), w_in[...], preferred_element_type=F32)
        return acc.reshape(4, n, 16, 256)

    def apply_chunk(u, prev, out, x0, lo, hi):
        acc = stencil(u, x0, lo, hi)
        px = pl.ds(x0 + 1, 4)
        v = u[px, lo:hi].astype(F32)
        d = (d0[pl.ds(x0, 4), lo - 1 : hi - 1] - centre) * inv_radius
        if prev is None:
            res = acc * (inv_radius / 72.0) + d * v
        else:
            res = acc * (inv_radius / 36.0) + (2.0 * d) * v - prev[px, lo:hi].astype(F32)
        out[px, lo:hi] = res.astype(BF16)

    def apply_step(u, prev, out, lo, hi):
        @pl.loop(0, 4, unroll=4)
        def _(i):
            apply_chunk(u, prev, out, 4 * i, lo, hi)

    def outside_zero(out):
        @pl.when(yy == 0)
        def _():
            out[:, 1] = jnp.zeros((18, 16, 256), BF16)

        @pl.when(yy == 3)
        def _():
            out[:, 10] = jnp.zeros((18, 16, 256), BF16)

    apply_step(u0, None, u1, 3, 9)

    def halo_wait(side):
        bulk(u0.at[1:17, 2], hal_r.at[side]).wait_recv()
        pot_edge(side).wait_recv()

    @pl.when(yy < 3)
    def _():
        halo_wait(0)

    @pl.when(yy > 0)
    def _():
        halo_wait(1)

    apply_step(u0, None, u1, 1, 3)
    apply_step(u0, None, u1, 9, 11)
    outside_zero(u1)
    apply_step(u1, u0, u2, 1, 11)
    outside_zero(u2)
    apply_step(u2, u1, u3, 1, 11)
    outside_zero(u3)
    apply_step(u3, u2, u4, 2, 10)

    def layer(side):
        far = rem(yy + 3 + 2 * side, 4)
        mine, theirs, lanes = (2, 10, pl.ds(0, 128)) if side == 0 else (9, 1, pl.ds(128, 128))
        return remote(
            u4.at[pl.ds(1, 16), mine, :, lanes],
            u4.at[pl.ds(1, 16), theirs, :, lanes],
            edge_s.at[side], edge_r.at[side], (sx, far * 4 + s4),
        )

    @pl.when(yy > 0)
    def _():
        layer(0).start()

    @pl.when(yy < 3)
    def _():
        layer(1).start()

    def send_out(src, dst, ss, rr, first):
        for k in (*OTHER, *PLANE, *FIRST):
            px, p4 = peer(k)
            remote(
                src.at[pl.ds(first + 2 * px, 2), pl.ds(2 * first + 2 * p4, 2)],
                dst.at[j], ss.at[0], rr.at[0], (px, yy * 4 + p4),
            ).start()

    send_out(u4, rf, f_s, f_r, 1)
    rf[j] = u4[xs, bs]

    @pl.when(yy < 3)
    def _():
        layer(0).wait_recv()

    @pl.when(yy > 0)
    def _():
        layer(1).wait_recv()

    zero = jnp.zeros((), BF16)

    @pl.loop(0, 2)
    def _(i):
        own, slab_p, slab_q, even_p, even_q = [], [], [], [], []
        first = lax.broadcasted_iota(jnp.int32, (8, 16, 128), 2) < 64
        last = lax.broadcasted_iota(jnp.int32, (8, 16, 128), 0) % 2 == 1
        for m in range(4):
            before, here, after = (u4.at[8 * i + 2 * m + n] for n in (1, 2, 3))
            own.append(after[2:10].reshape(128, 256))
            nxt = [u[3:11, :, 0:128] for u in (before, here, after)]
            slab_p.append(jnp.where(first & last, nxt[1], zero).reshape(128, 128))
            far = nxt[2] + jnp.where(last, nxt[0], zero)
            slab_q.append(jnp.where(first, far, after[1:9, :, 128:256]).reshape(128, 128))
            for b in (4, 6, 8, 10):
                even_p.append(jnp.where(first[0], before[b, :, 0:128], zero))
                even_q.append(jnp.where(first[0], here[b, :, 0:128], zero))
        join = lambda parts: jnp.concatenate(parts, axis=0)
        lhs = jnp.concatenate([join(own), join(slab_p), join(slab_q)], axis=1)
        acc = jnp.dot(lhs, w_in[256:768], preferred_element_type=F32) * (1.0 / 72.0)
        co[pl.ds(4 * i, 4)] = acc.astype(BF16).reshape(4, 8, 16, 256)
        lhs = jnp.concatenate([join(even_p), join(even_q)], axis=1)
        acc = jnp.dot(lhs, w_in[512:768, 128:256], preferred_element_type=F32) * (1.0 / 72.0)
        ce[pl.ds(4 * i, 4)] = acc.astype(BF16).reshape(4, 4, 16, 128)

    for k in (*OTHER, *PLANE, *FIRST):
        px, p4 = peer(k)
        dev = (px, yy * 4 + p4)
        remote(co.at[px, pl.ds(2 * p4, 2)], rco.at[j], i_s.at[0], i_r.at[0], dev).start()
        remote(ce.at[px, p4], rce.at[j], i_s.at[1], i_r.at[1], dev).start()
    rco[j] = co[sx, pl.ds(2 * s4, 2)]
    rce[j] = ce[sx, s4]

    units = [(a, b) for a in range(2) for b in range(2)]

    def flat(value):
        return value.reshape(-1, value.shape[-1])

    def core_copy(n, r):
        return remote(
            part.at[n, r, :, 1 - c], other.at[n, r], core_s.at[n, r], core_r.at[n, r], sibling
        )

    def give(n, r, g):
        g = g.reshape(2, 2, 2, 16, 512)
        gm[n, r] = g
        part[n, r] = g.astype(BF16)
        core_copy(n, r).start()

    def take(n, r):
        core_copy(n, r).wait_recv()
        half[n, r] = (gm[n, r, :, c] + other[n, r].astype(F32)).astype(BF16)

    def local_image():
        first = lax.broadcasted_iota(jnp.int32, (512, 128), 1) < 64
        for a, b in units:
            slabs = [flat(rf[:, n, b]) for n in (a, 1 - a)]
            for n in (a, 1 - a):
                if b == 0:
                    slabs.append(jnp.where(first, flat(rf[:, n, 1, :, 0:128]), zero))
                else:
                    slabs.append(jnp.where(first, zero, flat(rf[:, n, 0, :, 128:256])))
            acc = jnp.dot(jnp.concatenate(slabs, axis=1), w_in[...], preferred_element_type=F32)
            here = d0[2 * sx + a, 1 + 2 * s4 + b] * flat(rf[:, a, b]).astype(F32)
            ri[a, b] = (acc * (1.0 / 72.0) + here).astype(BF16)

    def nt(left, right):
        left, right = (jnp.concatenate(parts, axis=1) for parts in (left, right))
        return lax.dot_general(left, right, NT, preferred_element_type=F32)

    lanes_z = pl.ds(pl.multiple_of(128 * z, 128), 128)

    def margin_y_copy(dy):
        return remote(half.at[0, ys[dy]], ysum.at[dy], y_s.at[0], y_r.at[0], (sx, ys[dy] * 4 + s4))

    def margin_y_sum():
        total = half[0, yy].astype(F32)
        for dy in (1, 2, 3):
            total += ysum[dy].astype(F32)
        plane_part[...] = total.astype(BF16)

    def margin_plane_copy(k):
        dz, dx = k % 4, k // 4
        lanes = pl.ds(pl.multiple_of(128 * zs[dz], 128), 128)
        return remote(
            plane_part.at[xhs[dx], xls[dx], :, lanes], rs.at[0, k], rs_s.at[0], rs_r.at[0],
            (xls[dx] * 4 + zs[dz], yy * 4 + xhs[dx] * 2 + c),
        )

    def projected_copies(r, own):
        for k in range(1 if own else 0, 16):
            dz, dx = k % 4, k // 4
            lanes = pl.ds(pl.multiple_of(128 * zs[dz], 128), 128)
            remote(
                half.at[1, r, xhs[dx], xls[dx], :, lanes],
                rs.at[1, 16 * yy + 4 * x + z], rs_s.at[1], rs_r.at[1],
                (xls[dx] * 4 + zs[dz], r * 4 + xhs[dx] * 2 + c),
            ).start()

    bulk(t.at[1:GROUP], f_r.at[0]).wait_recv()
    field_rows = [flat(rf[:, a, b]) for a, b in units]
    for r in range(4):
        give(0, r, nt([v[128 * r : 128 * r + 128] for v in field_rows], field_rows))
    local_image()
    for r in range(4):
        take(0, r)
    for dy in (1, 2, 3):
        margin_y_copy(dy).start()
    for r in range(4):
        gm[1, r] = nt(
            [v[128 * r : 128 * r + 128] for v in field_rows], [ri[a, b] for a, b in units]
        ).reshape(2, 2, 2, 16, 512)
    bulk(t.at[1:GROUP, 0], i_r.at[0]).wait_recv()
    bulk(rs.at[1, 0 : GROUP - 1], i_r.at[1]).wait_recv()
    order = [rem(yy + 1 + i, 4) for i in range(4)]
    field = [rf[:, 1, 0], rf[:, 1, 1], rf[:, 0, 1, :, 128:256]]
    across = [rco[:, 0], rco[:, 1], rce[...]]
    right = [flat(v) for v in across + field]
    for r in order:
        eight = pl.ds(8 * r, 8)
        left = [rf[eight, 1, 0], rf[eight, 1, 1], rf[eight, 0, 1, :, 128:256]]
        left += [rco[eight, 0], rco[eight, 1], rce[eight]]
        give(1, r, nt([flat(v) for v in left], right) + gm[1, r].reshape(128, 512))
    for r in order:
        take(1, r)
        projected_copies(r, r is order[3])
    rs[1, 16 * yy + 4 * x + z] = half[1, yy, xh, xl, :, lanes_z]

    bulk(ysum.at[1:4], y_r.at[0]).wait_recv()
    margin_y_sum()
    for k in range(1, 16):
        margin_plane_copy(k).start()
    rs[0, 0] = plane_part[xh, xl, :, lanes_z]

    bulk(rs.at[0, 1:16], rs_r.at[0]).wait_recv()
    ob[sx, 0] = jnp.sum(rs[0, 0:16].astype(F32), axis=0) * (1.0 / 131072.0)
    bulk(rs.at[1, 0:63], rs_r.at[1]).wait_recv()
    ob[sx, 1] = jnp.sum(rs[1].astype(F32), axis=0) * (1.0 / 131072.0)

    for k in range(1, 8):
        far = rem(sx + k, 8)
        remote(ob.at[sx], ob.at[sx], ag_s.at[0], ag_r.at[0], (far, sy)).start()

    for sem in (in_s, f_s):
        bulk(t.at[1:GROUP], sem.at[0]).wait_send()
    bulk(t.at[1:GROUP, 0], i_s.at[0]).wait_send()
    bulk(rs.at[0, 1:GROUP], i_s.at[1]).wait_send()
    for stage, n in enumerate((3, 12, 16)):
        bulk(rs.at[0, 0:n], pin_s.at[stage]).wait_send()

    def sent(side):
        bulk(u0.at[1:17, 2], hal_s.at[side]).wait_send()
        pot_edge(side).wait_send()
        layer(side).wait_send()

    @pl.when(yy > 0)
    def _():
        sent(0)

    @pl.when(yy < 3)
    def _():
        sent(1)

    for r in range(4):
        core_copy(0, r).wait_send()
        core_copy(1, r).wait_send()
    bulk(ysum.at[1:4], y_s.at[0]).wait_send()
    bulk(rs.at[0, 1:16], rs_s.at[0]).wait_send()
    bulk(rs.at[1, 0:63], rs_s.at[1]).wait_send()
    bulk(ob.at[0:7], ag_s.at[0]).wait_send()
    bulk(ob.at[0:7], ag_r.at[0]).wait_recv()
    for s in range(8):
        rows, lanes = pl.ds(16 * (s // 4), 16), pl.ds(128 * (s % 4), 128)
        margin[rows, lanes] = ob[s, 0]
        projected[rows, lanes] = ob[s, 1]


def on_device(wave, potential, lower_cut, upper_edge):
    dma = pltpu.SemaphoreType.DMA
    field = pltpu.VMEM((18, 12, 16, 256), BF16)
    block = pltpu.VMEM((GROUP, 2, 2, 16, 256), BF16)
    vmem = pl.BlockSpec(memory_space=pltpu.VMEM)
    hbm = pl.BlockSpec(memory_space=pl.ANY)
    smem = pl.BlockSpec(memory_space=pltpu.SMEM)
    weights = jnp.asarray(stencil_matrix(), BF16)
    return pl.pallas_call(
        kernel,
        out_shape=[jax.ShapeDtypeStruct((32, 512), F32)] * 2,
        in_specs=[hbm, hbm, smem, smem, hbm],
        out_specs=[vmem, vmem],
        scratch_shapes=[
            pltpu.VMEM(wave.shape, BF16),
            pltpu.VMEM(potential.shape, F32),
            pltpu.VMEM(weights.shape, BF16),
            block,
            field, field, field, field, field,
            pltpu.VMEM((8, 8, 16, 256), BF16),
            pltpu.VMEM((8, 4, 16, 128), BF16),
            pltpu.VMEM((16, 10, 1, 256), F32),
            block,
            pltpu.VMEM((GROUP, 2, 16, 256), BF16),
            pltpu.VMEM((GROUP, 16, 128), BF16),
            pltpu.VMEM((2, 2, 512, 256), BF16),
            pltpu.VMEM((2, 4, 2, 2, 2, 16, 512), F32),
            pltpu.VMEM((2, 4, 2, 2, 2, 16, 512), BF16),
            pltpu.VMEM((2, 4, 2, 2, 16, 512), BF16),
            pltpu.VMEM((2, 4, 2, 2, 16, 512), BF16),
            pltpu.VMEM((4, 2, 2, 16, 512), BF16),
            pltpu.VMEM((2, 2, 16, 512), BF16),
            pltpu.VMEM((2, 64, 16, 128), BF16),
            pltpu.VMEM((8, 2, 16, 128), F32),
            dma((3,)), dma((1,)), dma((32,)), dma((3,)), dma((3,)),
            dma((2,)), dma((2,)), dma((2,)), dma((2,)),
            dma((2,)), dma((2,)),
            dma((1,)), dma((1,)), dma((2,)), dma((2,)),
            dma((2, 4)), dma((2, 4)), dma((1,)), dma((1,)), dma((2,)), dma((2,)),
            dma((1,)), dma((1,)),
            pltpu.SemaphoreType.REGULAR, pltpu.SemaphoreType.REGULAR,
        ],
        compiler_params=pltpu.CompilerParams(
            collective_id=0, has_side_effects=True, vmem_limit_bytes=127 << 19
        ),
    )(wave, potential, lower_cut, upper_edge, weights)


def solution(mesh):
    return jax.shard_map(
        on_device,
        mesh=mesh,
        in_specs=(P("sx", "sy", None, None), P("sx", "sy", None), P(), P()),
        out_specs=(P("sy", None), P("sy", None)),
        check_vma=False,
    )
```

```python
import functools

import jax
import jax.numpy as jnp
import numpy as np
from jax import lax
from jax.experimental import pallas as pl
from jax.experimental.pallas import tpu as pltpu
from jax.sharding import PartitionSpec as P

MESH = pl.DeviceIdType.MESH
F32, BF16 = jnp.float32, jnp.bfloat16
GROUP = 32
FIRST = (2, 8, 1, 3, 4, 12)
PLANE = (10, 6, 14, 9, 11, 5, 7, 13, 15)
OTHER = (26, 22, 30, 25, 27, 18, 24, 21, 23, 29, 31, 17, 19, 20, 28, 16)
NT = (((1,), (1,)), ((), ()))


def stencil_matrix():
    my, ky = np.zeros((4, 6)), np.zeros((4, 6))
    for i in range(4):
        my[i, i : i + 3] = 1, 4, 1
        ky[i, i : i + 3] = -1, 2, -1
    mz, kz = np.zeros((64, 64)), np.zeros((64, 64))
    for i in range(64):
        for j in range(max(i - 1, 0), min(i + 2, 64)):
            mz[i, j] = 4 if i == j else 1
            kz[i, j] = 2 if i == j else -1
    m = np.einsum("ij,kl->jlik", my, mz).reshape(6, 64, 256)
    g = np.einsum("ij,kl->jlik", ky, mz) + np.einsum("ij,kl->jlik", my, kz)
    g = g.reshape(6, 64, 256)
    p, q = 2 * m + 4 * g, g - m
    own = lambda t: t[1:5].reshape(256, 256)
    edge = lambda t: np.concatenate([t[5], t[0]], axis=0)
    return np.concatenate([own(p), own(q), edge(p), edge(q)], axis=0)


def kernel(
    wave_hbm, pot_hbm, low, high, w_hbm, summed,
    wave, pot, w_in, t, u0, u1, u2, u3, u4, face, d0, rf, faces, ri, gm, part, other, half, ysum, plane_part, rs, ob,
    load, in_s, in_r, pin_s, pin_r, hal_s, hal_r, phal_s, phal_r, edge_s, edge_r,
    f_s, f_r, i_s, i_r, core_s, core_r, y_s, y_r, rs_s, rs_r, ag_s, ag_r, plane, chip,
):
    loads = [
        pltpu.make_async_copy(src, dst, load.at[i])
        for i, (src, dst) in enumerate([(wave_hbm, wave), (pot_hbm, pot), (w_hbm, w_in)])
    ]
    for copy in loads:
        copy.start()

    sx, sy = lax.axis_index("sx"), lax.axis_index("sy")
    rem, div = lax.rem, lax.div
    xl, z, yy, s4 = div(sx, 4), rem(sx, 4), div(sy, 4), rem(sy, 4)
    xh, c = div(s4, 2), rem(s4, 2)
    x = 2 * xh + xl
    j = sx * 4 + s4

    turn = [None, 1 + 2 * c, 2, 3 - 2 * c]
    zs = [z] + [rem(z + turn[d], 4) for d in (1, 2, 3)]
    xt = [x] + [rem(x + turn[d], 4) for d in (1, 2, 3)]
    ys = [yy] + [rem(yy + turn[d], 4) for d in (1, 2, 3)]
    xls, xhs, cs = [rem(v, 2) for v in xt], [div(v, 2) for v in xt], [c, 1 - c]
    def peer(k):
        dz, dx, dc = k % 4, (k // 4) % 4, k // 16
        return xls[dx] * 4 + zs[dz], xhs[dx] * 2 + cs[dc]

    def remote(src, dst, ss, rr, dev):
        return pltpu.make_async_remote_copy(
            src_ref=src, dst_ref=dst, send_sem=ss, recv_sem=rr, device_id=dev, device_id_type=MESH
        )

    sibling = (sx, sy + 1 - 2 * c)

    def bulk(ref, sem):
        return remote(ref, ref, sem, sem, sibling)

    for u in (u0, u1, u2, u3, u4):
        u[0] = jnp.zeros(u.shape[1:], BF16)
        u[17] = jnp.zeros(u.shape[1:], BF16)
        for b in (0, 1, 10, 11):
            u[:, b] = jnp.zeros((18, 16, 256), BF16)
    d0[:, 0] = jnp.zeros((16, 1, 256), F32)
    d0[:, 9] = jnp.zeros((16, 1, 256), F32)

    barrier = pltpu.get_barrier_semaphore()
    direct = [(px, yy * 4 + p4) for px, p4 in (peer(k) for k in (1, 2, 3, 4, 8, 12, 16))]
    direct += [(sx, ys[dy] * 4 + s4) for dy in (1, 2, 3)]
    for dev in direct:
        pl.semaphore_signal(barrier, inc=1, device_id=dev, device_id_type=MESH)

    eye = (
        lax.broadcasted_iota(jnp.int32, (256, 256), 0)
        == lax.broadcasted_iota(jnp.int32, (256, 256), 1)
    ).astype(F32).astype(BF16)
    loads[0].wait()
    loads[1].wait()
    for a in range(2):
        for b in range(2):
            nodes = wave[a, 4 * b : 4 * b + 4].reshape(256, 512)
            for h in range(2):
                turned = lax.dot_general(
                    eye, nodes[:, 256 * h : 256 * h + 256], NT, preferred_element_type=F32
                )
                t[16 * h : 16 * h + 16, a, b] = turned.astype(BF16).reshape(16, 16, 256)
            d0[2 * sx + a, 1 + 2 * s4 + b] = jnp.concatenate(
                [pot[a, 4 * b + i : 4 * b + i + 1, :] for i in range(4)], axis=1
            )

    pl.semaphore_wait(barrier, len(direct))

    xs = pl.ds(1 + 2 * sx, 2)
    bs = pl.ds(2 + 2 * s4, 2)
    own_pot = d0.at[pl.ds(2 * sx, 2), pl.ds(1 + 2 * s4, 2)]

    def in_copy(k):
        px, p4 = peer(k)
        return remote(
            t.at[px * 4 + p4], u0.at[xs, bs], in_s.at[0], in_r.at[j], (px, yy * 4 + p4)
        )

    def send_in(ks):
        for k in ks:
            in_copy(k).start()

    def send_pot(strip, stage, devs):
        for dev in devs:
            remote(strip, strip, pin_s.at[stage], pin_r.at[stage], dev).start()

    along_z, along_x = direct[0:3], direct[3:6]
    for dev in along_z:
        pl.semaphore_signal(plane, inc=1, device_id=dev, device_id_type=MESH)
    send_pot(own_pot, 0, along_z)
    send_in(FIRST)
    pl.semaphore_wait(plane, 3)
    pl.semaphore_signal(chip, inc=1, device_id=sibling, device_id_type=MESH)
    bulk(rs.at[0, 0:3], pin_r.at[0]).wait_recv()
    send_pot(d0.at[pl.ds(8 * xl, 8), pl.ds(1 + 2 * s4, 2)], 1, along_x)
    send_in(PLANE)
    pl.semaphore_wait(chip, 1)
    send_in(OTHER)
    bulk(rs.at[0, 0:12], pin_r.at[1]).wait_recv()
    for q in (c, 2 + c):
        send_pot(d0.at[:, pl.ds(1 + 2 * q, 2)], 2, [sibling])

    u0[xs, bs] = t[j]

    def edge_ends(side):
        far = rem(yy + 3 + 2 * side, 4)
        return ((2, 10) if side == 0 else (9, 1)) + ((sx, far * 4 + s4),)

    def send_on(s, quarter):
        side = quarter // 3
        mine, theirs, dev = edge_ends(side)
        ux = pl.ds(1 + 2 * s, 2)

        @pl.when(yy > 0 if side == 0 else yy < 3)
        def _():
            remote(u0.at[ux, mine], u0.at[ux, theirs], hal_s.at[side], hal_r.at[side], dev).start()

    def pot_edge(side):
        mine, theirs, dev = edge_ends(side)
        return remote(
            d0.at[:, mine - 1], d0.at[:, theirs - 1], phal_s.at[side], phal_r.at[side], dev
        )

    bulk(rs.at[0, 0:16], pin_r.at[2]).wait_recv()

    @pl.when(yy > 0)
    def _():
        pot_edge(0).start()

    @pl.when(yy < 3)
    def _():
        pot_edge(1).start()

    def arrived(i):
        @pl.when(j != i)
        def _():
            bulk(u0.at[xs, bs], in_r.at[i]).wait_recv()

    for s in range(8):
        for quarter in (0, 3):
            arrived(4 * s + quarter)
            send_on(s, quarter)
    for s in range(8):
        for quarter in (1, 2):
            arrived(4 * s + quarter)

    loads[2].wait()
    centre = 0.5 * (high[0] + low[0])
    inv_radius = 1.0 / (0.5 * (high[0] - low[0]))

    def edge_slab(nxt, prv):
        return jnp.where(lax.broadcasted_iota(jnp.int32, nxt.shape, len(nxt.shape) - 1) < 64, nxt, prv)

    def stencil(u, x0, lo, hi):
        n = hi - lo
        rows = 4 * n * 16
        mid = u[pl.ds(x0 + 1, 4), lo - 1 : hi + 1]
        beside = u[pl.ds(x0, 4), lo - 1 : hi + 1] + u[pl.ds(x0 + 2, 4), lo - 1 : hi + 1]
        slabs = [v[:, 1 : n + 1].reshape(rows, 256) for v in (mid, beside)]
        slabs += [
            edge_slab(v[:, 2:, :, 0:128], v[:, :n, :, 128:256]).reshape(rows, 128)
            for v in (mid, beside)
        ]
        acc = jnp.dot(jnp.concatenate(slabs, axis=1), w_in[...], preferred_element_type=F32)
        return acc.reshape(4, n, 16, 256)

    def apply_chunk(u, prev, out, x0, lo, hi):
        acc = stencil(u, x0, lo, hi)
        px = pl.ds(x0 + 1, 4)
        v = u[px, lo:hi].astype(F32)
        d = (d0[pl.ds(x0, 4), lo - 1 : hi - 1] - centre) * inv_radius
        if prev is None:
            res = acc * (inv_radius / 72.0) + d * v
        else:
            res = acc * (inv_radius / 36.0) + (2.0 * d) * v - prev[px, lo:hi].astype(F32)
        out[px, lo:hi] = res.astype(BF16)

    def apply_step(u, prev, out, lo, hi):
        @pl.loop(0, 4, unroll=4)
        def _(i):
            apply_chunk(u, prev, out, 4 * i, lo, hi)

    def outside_zero(out):
        @pl.when(yy == 0)
        def _():
            out[:, 1] = jnp.zeros((18, 16, 256), BF16)

        @pl.when(yy == 3)
        def _():
            out[:, 10] = jnp.zeros((18, 16, 256), BF16)

    apply_step(u0, None, u1, 3, 9)
    apply_step(u1, u0, u2, 4, 8)

    def halo_wait(side):
        bulk(u0.at[1:17, 2], hal_r.at[side]).wait_recv()
        pot_edge(side).wait_recv()

    @pl.when(yy < 3)
    def _():
        halo_wait(0)

    @pl.when(yy > 0)
    def _():
        halo_wait(1)

    apply_step(u0, None, u1, 1, 3)
    apply_step(u0, None, u1, 9, 11)
    outside_zero(u1)
    apply_step(u1, u0, u2, 1, 4)
    apply_step(u1, u0, u2, 8, 11)
    outside_zero(u2)
    apply_step(u2, u1, u3, 1, 11)
    outside_zero(u3)
    def send_out(ks):
        for k in ks:
            px, p4 = peer(k)
            remote(
                u4.at[pl.ds(1 + 2 * px, 2), pl.ds(2 + 2 * p4, 2)],
                rf.at[j], f_s.at[0], f_r.at[0], (px, yy * 4 + p4),
            ).start()

    far_order = (*OTHER, *PLANE, *FIRST)
    for h, parity in ((1 - xl, 1), (xl, 0)):
        for i in range(2):
            apply_chunk(u3, u2, u4, 8 * h + 4 * i, 2, 10)
        send_out([k for k in far_order if (k // 4) % 2 == parity])

    def layer(side):
        far = rem(yy + 3 + 2 * side, 4)
        mine, theirs, lanes = (2, 10, pl.ds(0, 128)) if side == 0 else (9, 1, pl.ds(128, 128))
        return remote(
            u4.at[pl.ds(1, 16), mine, :, lanes],
            u4.at[pl.ds(1, 16), theirs, :, lanes],
            edge_s.at[side], edge_r.at[side], (sx, far * 4 + s4),
        )

    @pl.when(yy > 0)
    def _():
        layer(0).start()

    @pl.when(yy < 3)
    def _():
        layer(1).start()

    rf[j] = u4[xs, bs]

    @pl.when(yy < 3)
    def _():
        layer(0).wait_recv()

    @pl.when(yy > 0)
    def _():
        layer(1).wait_recv()

    zero = jnp.zeros((), BF16)

    @pl.loop(0, 2)
    def _(i):
        own, slab_p, slab_q, even_p, even_q = [], [], [], [], []
        first = lax.broadcasted_iota(jnp.int32, (8, 16, 128), 2) < 64
        last = lax.broadcasted_iota(jnp.int32, (8, 16, 128), 0) % 2 == 1
        for m in range(4):
            before, here, after = (u4.at[8 * i + 2 * m + n] for n in (1, 2, 3))
            own.append(after[2:10].reshape(128, 256))
            nxt = [u[3:11, :, 0:128] for u in (before, here, after)]
            slab_p.append(jnp.where(first & last, nxt[1], zero).reshape(128, 128))
            far = nxt[2] + jnp.where(last, nxt[0], zero)
            slab_q.append(jnp.where(first, far, after[1:9, :, 128:256]).reshape(128, 128))
            for b in (4, 6, 8, 10):
                even_p.append(jnp.where(first[0], before[b, :, 0:128], zero))
                even_q.append(jnp.where(first[0], here[b, :, 0:128], zero))
        join = lambda parts: jnp.concatenate(parts, axis=0)
        lhs = jnp.concatenate([join(own), join(slab_p), join(slab_q)], axis=1)
        acc = jnp.dot(lhs, w_in[256:768], preferred_element_type=F32) * (1.0 / 72.0)
        odd = acc.astype(BF16).reshape(4, 4, 2, 16, 256)
        for n in range(4):
            face[pl.ds(4 * i, 4), :, n] = odd[:, :, n // 2, :, 128 * (n % 2) : 128 * (n % 2) + 128]
        lhs = jnp.concatenate([join(even_p), join(even_q)], axis=1)
        acc = jnp.dot(lhs, w_in[512:768, 128:256], preferred_element_type=F32) * (1.0 / 72.0)
        face[pl.ds(4 * i, 4), :, 4] = acc.astype(BF16).reshape(4, 4, 16, 128)

    for k in (*OTHER, *PLANE, *FIRST):
        px, p4 = peer(k)
        dev = (px, yy * 4 + p4)
        remote(face.at[px, p4], faces.at[j], i_s.at[0], i_r.at[0], dev).start()
    faces[j] = face[sx, s4]

    units = [(a, b) for a in range(2) for b in range(2)]

    def flat(value):
        return value.reshape(-1, value.shape[-1])

    def core_copy(n, r):
        return remote(
            part.at[n, r, :, 1 - c], other.at[n, r], core_s.at[n, r], core_r.at[n, r], sibling
        )

    def give(n, r, g):
        g = g.reshape(2, 2, 2, 16, 512)
        gm[n, r] = g
        part[n, r] = g.astype(BF16)
        core_copy(n, r).start()

    def take(n, r):
        core_copy(n, r).wait_recv()
        half[n, r] = (gm[n, r, :, c] + other[n, r].astype(F32)).astype(BF16)

    def local_image():
        first = lax.broadcasted_iota(jnp.int32, (512, 128), 1) < 64
        for a, b in units:
            slabs = [flat(rf[:, n, b]) for n in (a, 1 - a)]
            for n in (a, 1 - a):
                if b == 0:
                    slabs.append(jnp.where(first, flat(rf[:, n, 1, :, 0:128]), zero))
                else:
                    slabs.append(jnp.where(first, zero, flat(rf[:, n, 0, :, 128:256])))
            acc = jnp.dot(jnp.concatenate(slabs, axis=1), w_in[...], preferred_element_type=F32)
            here = d0[2 * sx + a, 1 + 2 * s4 + b] * flat(rf[:, a, b]).astype(F32)
            ri[a, b] = (acc * (1.0 / 72.0) + here).astype(BF16)

    def nt(left, right):
        left, right = (jnp.concatenate(parts, axis=1) for parts in (left, right))
        return lax.dot_general(left, right, NT, preferred_element_type=F32)

    lanes_z = pl.ds(pl.multiple_of(128 * z, 128), 128)

    def margin_y_copy(dy):
        return remote(half.at[0, ys[dy]], ysum.at[dy], y_s.at[0], y_r.at[0], (sx, ys[dy] * 4 + s4))

    def margin_y_sum():
        total = half[0, yy].astype(F32)
        for dy in (1, 2, 3):
            total += ysum[dy].astype(F32)
        plane_part[...] = total.astype(BF16)

    def margin_plane_copy(k):
        dz, dx = k % 4, k // 4
        lanes = pl.ds(pl.multiple_of(128 * zs[dz], 128), 128)
        return remote(
            plane_part.at[xhs[dx], xls[dx], :, lanes], rs.at[0, k], rs_s.at[0], rs_r.at[0],
            (xls[dx] * 4 + zs[dz], yy * 4 + xhs[dx] * 2 + c),
        )

    def projected_copies(r, own):
        for k in range(1 if own else 0, 16):
            dz, dx = k % 4, k // 4
            lanes = pl.ds(pl.multiple_of(128 * zs[dz], 128), 128)
            remote(
                half.at[1, r, xhs[dx], xls[dx], :, lanes],
                rs.at[1, 16 * yy + 4 * x + z], rs_s.at[1], rs_r.at[1],
                (xls[dx] * 4 + zs[dz], r * 4 + xhs[dx] * 2 + c),
            ).start()

    bulk(t.at[1:GROUP], f_r.at[0]).wait_recv()
    field_rows = [flat(rf[:, a, b]) for a, b in units]
    for r in range(4):
        give(0, r, nt([v[128 * r : 128 * r + 128] for v in field_rows], field_rows))
    local_image()
    for r in range(4):
        take(0, r)
    for dy in (1, 2, 3):
        margin_y_copy(dy).start()
    for r in range(4):
        gm[1, r] = nt(
            [v[128 * r : 128 * r + 128] for v in field_rows], [ri[a, b] for a, b in units]
        ).reshape(2, 2, 2, 16, 512)
    bulk(faces.at[1:GROUP], i_r.at[0]).wait_recv()
    order = [rem(yy + 1 + i, 4) for i in range(4)]
    def field(js):
        return [flat(v) for v in (rf[js, 1, 0], rf[js, 1, 1], rf[js, 0, 1, :, 128:256])]

    def across(js):
        return [flat(faces[js, n]) for n in range(5)]

    every = slice(None)
    right = across(every) + field(every)
    for r in order:
        eight = pl.ds(8 * r, 8)
        give(1, r, nt(field(eight) + across(eight), right) + gm[1, r].reshape(128, 512))
    for r in order:
        take(1, r)
        projected_copies(r, r is order[3])
    rs[1, 16 * yy + 4 * x + z] = half[1, yy, xh, xl, :, lanes_z]

    bulk(ysum.at[1:4], y_r.at[0]).wait_recv()
    margin_y_sum()
    for k in range(1, 16):
        margin_plane_copy(k).start()
    rs[0, 0] = plane_part[xh, xl, :, lanes_z]

    bulk(rs.at[0, 1:16], rs_r.at[0]).wait_recv()
    ob[sx, 0] = jnp.sum(rs[0, 0:16].astype(F32), axis=0)
    bulk(rs.at[1, 0:63], rs_r.at[1]).wait_recv()
    ob[sx, 1] = jnp.sum(rs[1].astype(F32), axis=0)

    for k in range(1, 8):
        far = rem(sx + k, 8)
        remote(ob.at[sx], ob.at[sx], ag_s.at[0], ag_r.at[0], (far, sy)).start()

    for sem in (in_s, f_s):
        bulk(t.at[1:GROUP], sem.at[0]).wait_send()
    bulk(faces.at[1:GROUP], i_s.at[0]).wait_send()
    for stage, n in enumerate((3, 12, 16)):
        bulk(rs.at[0, 0:n], pin_s.at[stage]).wait_send()

    def sent(side):
        bulk(u0.at[1:17, 2], hal_s.at[side]).wait_send()
        pot_edge(side).wait_send()
        layer(side).wait_send()

    @pl.when(yy > 0)
    def _():
        sent(0)

    @pl.when(yy < 3)
    def _():
        sent(1)

    for r in range(4):
        core_copy(0, r).wait_send()
        core_copy(1, r).wait_send()
    bulk(ysum.at[1:4], y_s.at[0]).wait_send()
    bulk(rs.at[0, 1:16], rs_s.at[0]).wait_send()
    bulk(rs.at[1, 0:63], rs_s.at[1]).wait_send()
    bulk(ob.at[0:7], ag_s.at[0]).wait_send()
    bulk(ob.at[0:7], ag_r.at[0]).wait_recv()
    for s in range(8):
        rows, lanes = pl.ds(16 * (s // 4), 16), pl.ds(128 * (s % 4), 128)
        summed[0, rows, lanes] = ob[s, 0]
        summed[1, rows, lanes] = ob[s, 1]


def on_device(wave, potential, lower_cut, upper_edge):
    dma = pltpu.SemaphoreType.DMA
    field = pltpu.VMEM((18, 12, 16, 256), BF16)
    block = pltpu.VMEM((GROUP, 2, 2, 16, 256), BF16)
    vmem = pl.BlockSpec(memory_space=pltpu.VMEM)
    hbm = pl.BlockSpec(memory_space=pl.ANY)
    smem = pl.BlockSpec(memory_space=pltpu.SMEM)
    weights = jnp.asarray(stencil_matrix(), BF16)
    summed = pl.pallas_call(
        kernel,
        out_shape=jax.ShapeDtypeStruct((2, 32, 512), F32),
        in_specs=[hbm, hbm, smem, smem, hbm],
        out_specs=vmem,
        scratch_shapes=[
            pltpu.VMEM(wave.shape, BF16),
            pltpu.VMEM(potential.shape, F32),
            pltpu.VMEM(weights.shape, BF16),
            block,
            field, field, field, field, field,
            pltpu.VMEM((8, 4, 5, 16, 128), BF16),
            pltpu.VMEM((16, 10, 1, 256), F32),
            block,
            pltpu.VMEM((GROUP, 5, 16, 128), BF16),
            pltpu.VMEM((2, 2, 512, 256), BF16),
            pltpu.VMEM((2, 4, 2, 2, 2, 16, 512), F32),
            pltpu.VMEM((2, 4, 2, 2, 2, 16, 512), BF16),
            pltpu.VMEM((2, 4, 2, 2, 16, 512), BF16),
            pltpu.VMEM((2, 4, 2, 2, 16, 512), BF16),
            pltpu.VMEM((4, 2, 2, 16, 512), BF16),
            pltpu.VMEM((2, 2, 16, 512), BF16),
            pltpu.VMEM((2, 64, 16, 128), BF16),
            pltpu.VMEM((8, 2, 16, 128), F32),
            dma((3,)), dma((1,)), dma((32,)), dma((3,)), dma((3,)),
            dma((2,)), dma((2,)), dma((2,)), dma((2,)),
            dma((2,)), dma((2,)),
            dma((1,)), dma((1,)), dma((1,)), dma((1,)),
            dma((2, 4)), dma((2, 4)), dma((1,)), dma((1,)), dma((2,)), dma((2,)),
            dma((1,)), dma((1,)),
            pltpu.SemaphoreType.REGULAR, pltpu.SemaphoreType.REGULAR,
        ],
        compiler_params=pltpu.CompilerParams(
            collective_id=0, has_side_effects=True, vmem_limit_bytes=127 << 19
        ),
    )(wave, potential, lower_cut, upper_edge, weights)
    return summed[0] * (1.0 / 131072.0), summed[1] * (1.0 / 131072.0)


def solution(mesh):
    return jax.shard_map(
        on_device,
        mesh=mesh,
        in_specs=(P("sx", "sy", None, None), P("sx", "sy", None), P(), P()),
        out_specs=(P("sy", None), P("sy", None)),
        check_vma=False,
    )
```

```python
import functools

import jax
import jax.numpy as jnp
import numpy as np
from jax import lax
from jax.experimental import pallas as pl
from jax.experimental.pallas import tpu as pltpu
from jax.sharding import PartitionSpec as P

MESH = pl.DeviceIdType.MESH
F32, BF16 = jnp.float32, jnp.bfloat16
GROUP = 32
FIRST = (2, 8, 1, 3, 4, 12)
PLANE = (10, 6, 14, 9, 11, 5, 7, 13, 15)
OTHER = (26, 22, 30, 25, 27, 18, 24, 21, 23, 29, 31, 17, 19, 20, 28, 16)
NT = (((1,), (1,)), ((), ()))


def stencil_matrix():
    my, ky = np.zeros((4, 6)), np.zeros((4, 6))
    for i in range(4):
        my[i, i : i + 3] = 1, 4, 1
        ky[i, i : i + 3] = -1, 2, -1
    mz, kz = np.zeros((64, 64)), np.zeros((64, 64))
    for i in range(64):
        for j in range(max(i - 1, 0), min(i + 2, 64)):
            mz[i, j] = 4 if i == j else 1
            kz[i, j] = 2 if i == j else -1
    m = np.einsum("ij,kl->jlik", my, mz).reshape(6, 64, 256)
    g = np.einsum("ij,kl->jlik", ky, mz) + np.einsum("ij,kl->jlik", my, kz)
    g = g.reshape(6, 64, 256)
    p, q = 2 * m + 4 * g, g - m
    own = lambda t: t[1:5].reshape(256, 256)
    edge = lambda t: np.concatenate([t[5], t[0]], axis=0)
    return np.concatenate([own(p), own(q), edge(p), edge(q)], axis=0)


def kernel(
    wave_hbm, pot_hbm, low, high, w_hbm, summed,
    wave, pot, w_in, t, u0, u1, u2, u3, u4, face, d0, rf, faces, ri, gm, part, other, half, ysum, plane_part, rs, ob,
    load, in_s, in_r, pin_s, pin_r, hal_s, hal_r, phal_s, phal_r, edge_s, edge_r,
    f_s, f_r, i_s, i_r, core_s, core_r, y_s, y_r, rs_s, rs_r, ag_s, ag_r, plane, chip,
):
    loads = [
        pltpu.make_async_copy(src, dst, load.at[i])
        for i, (src, dst) in enumerate([(wave_hbm, wave), (pot_hbm, pot), (w_hbm, w_in)])
    ]
    for copy in loads:
        copy.start()

    sx, sy = lax.axis_index("sx"), lax.axis_index("sy")
    rem, div = lax.rem, lax.div
    xl, z, yy, s4 = div(sx, 4), rem(sx, 4), div(sy, 4), rem(sy, 4)
    xh, c = div(s4, 2), rem(s4, 2)
    x = 2 * xh + xl
    j = sx * 4 + s4

    turn = [None, 1 + 2 * c, 2, 3 - 2 * c]
    zs = [z] + [rem(z + turn[d], 4) for d in (1, 2, 3)]
    xt = [x] + [rem(x + turn[d], 4) for d in (1, 2, 3)]
    ys = [yy] + [rem(yy + turn[d], 4) for d in (1, 2, 3)]
    xls, xhs, cs = [rem(v, 2) for v in xt], [div(v, 2) for v in xt], [c, 1 - c]
    def peer(k):
        dz, dx, dc = k % 4, (k // 4) % 4, k // 16
        return xls[dx] * 4 + zs[dz], xhs[dx] * 2 + cs[dc]

    def remote(src, dst, ss, rr, dev):
        return pltpu.make_async_remote_copy(
            src_ref=src, dst_ref=dst, send_sem=ss, recv_sem=rr, device_id=dev, device_id_type=MESH
        )

    sibling = (sx, sy + 1 - 2 * c)

    def bulk(ref, sem):
        return remote(ref, ref, sem, sem, sibling)

    for u in (u0, u1, u2, u3, u4):
        u[0] = jnp.zeros(u.shape[1:], BF16)
        u[17] = jnp.zeros(u.shape[1:], BF16)
        for b in (0, 1, 10, 11):
            u[:, b] = jnp.zeros((18, 16, 256), BF16)
    d0[:, 0] = jnp.zeros((16, 1, 256), F32)
    d0[:, 9] = jnp.zeros((16, 1, 256), F32)

    barrier = pltpu.get_barrier_semaphore()
    direct = [(px, yy * 4 + p4) for px, p4 in (peer(k) for k in (1, 2, 3, 4, 8, 12, 16))]
    direct += [(sx, ys[dy] * 4 + s4) for dy in (1, 2, 3)]
    for dev in direct:
        pl.semaphore_signal(barrier, inc=1, device_id=dev, device_id_type=MESH)

    eye = (
        lax.broadcasted_iota(jnp.int32, (256, 256), 0)
        == lax.broadcasted_iota(jnp.int32, (256, 256), 1)
    ).astype(F32).astype(BF16)
    loads[0].wait()
    loads[1].wait()
    for a in range(2):
        for b in range(2):
            nodes = wave[a, 4 * b : 4 * b + 4].reshape(256, 512)
            for h in range(2):
                turned = lax.dot_general(
                    eye, nodes[:, 256 * h : 256 * h + 256], NT, preferred_element_type=F32
                )
                t[16 * h : 16 * h + 16, a, b] = turned.astype(BF16).reshape(16, 16, 256)
            d0[2 * sx + a, 1 + 2 * s4 + b] = jnp.concatenate(
                [pot[a, 4 * b + i : 4 * b + i + 1, :] for i in range(4)], axis=1
            )

    pl.semaphore_wait(barrier, len(direct))

    xs = pl.ds(1 + 2 * sx, 2)
    bs = pl.ds(2 + 2 * s4, 2)
    own_pot = d0.at[pl.ds(2 * sx, 2), pl.ds(1 + 2 * s4, 2)]

    def in_copy(k):
        px, p4 = peer(k)
        return remote(
            t.at[px * 4 + p4], u0.at[xs, bs], in_s.at[0], in_r.at[j], (px, yy * 4 + p4)
        )

    def send_in(ks):
        for k in ks:
            in_copy(k).start()

    def send_pot(strip, stage, devs):
        for dev in devs:
            remote(strip, strip, pin_s.at[stage], pin_r.at[stage], dev).start()

    along_z, along_x = direct[0:3], direct[3:6]
    for dev in along_z:
        pl.semaphore_signal(plane, inc=1, device_id=dev, device_id_type=MESH)
    send_pot(own_pot, 0, along_z)
    send_in(FIRST)
    pl.semaphore_wait(plane, 3)
    pl.semaphore_signal(chip, inc=1, device_id=sibling, device_id_type=MESH)
    bulk(rs.at[0, 0:3], pin_r.at[0]).wait_recv()
    send_pot(d0.at[pl.ds(8 * xl, 8), pl.ds(1 + 2 * s4, 2)], 1, along_x)
    send_in(PLANE)
    pl.semaphore_wait(chip, 1)
    send_in(OTHER)
    bulk(rs.at[0, 0:12], pin_r.at[1]).wait_recv()
    for q in (c, 2 + c):
        send_pot(d0.at[:, pl.ds(1 + 2 * q, 2)], 2, [sibling])

    u0[xs, bs] = t[j]

    def edge_ends(side):
        far = rem(yy + 3 + 2 * side, 4)
        return ((2, 10) if side == 0 else (9, 1)) + ((sx, far * 4 + s4),)

    def send_on(s, quarter):
        side = quarter // 3
        mine, theirs, dev = edge_ends(side)
        ux = pl.ds(1 + 2 * s, 2)

        @pl.when(yy > 0 if side == 0 else yy < 3)
        def _():
            remote(u0.at[ux, mine], u0.at[ux, theirs], hal_s.at[side], hal_r.at[side], dev).start()

    def pot_edge(side):
        mine, theirs, dev = edge_ends(side)
        return remote(
            d0.at[:, mine - 1], d0.at[:, theirs - 1], phal_s.at[side], phal_r.at[side], dev
        )

    bulk(rs.at[0, 0:16], pin_r.at[2]).wait_recv()

    @pl.when(yy > 0)
    def _():
        pot_edge(0).start()

    @pl.when(yy < 3)
    def _():
        pot_edge(1).start()

    def arrived(i):
        @pl.when(j != i)
        def _():
            bulk(u0.at[xs, bs], in_r.at[i]).wait_recv()

    for s in range(8):
        for quarter in (0, 3):
            arrived(4 * s + quarter)
            send_on(s, quarter)
    for s in range(8):
        for quarter in (1, 2):
            arrived(4 * s + quarter)

    loads[2].wait()
    centre = 0.5 * (high[0] + low[0])
    inv_radius = 1.0 / (0.5 * (high[0] - low[0]))

    def edge_slab(nxt, prv):
        return jnp.where(lax.broadcasted_iota(jnp.int32, nxt.shape, len(nxt.shape) - 1) < 64, nxt, prv)

    def stencil(u, x0, lo, hi):
        n = hi - lo
        rows = 4 * n * 16
        mid = u[pl.ds(x0 + 1, 4), lo - 1 : hi + 1]
        beside = u[pl.ds(x0, 4), lo - 1 : hi + 1] + u[pl.ds(x0 + 2, 4), lo - 1 : hi + 1]
        slabs = [v[:, 1 : n + 1].reshape(rows, 256) for v in (mid, beside)]
        slabs += [
            edge_slab(v[:, 2:, :, 0:128], v[:, :n, :, 128:256]).reshape(rows, 128)
            for v in (mid, beside)
        ]
        acc = jnp.dot(jnp.concatenate(slabs, axis=1), w_in[...], preferred_element_type=F32)
        return acc.reshape(4, n, 16, 256)

    def apply_chunk(u, prev, out, x0, lo, hi):
        acc = stencil(u, x0, lo, hi)
        px = pl.ds(x0 + 1, 4)
        v = u[px, lo:hi].astype(F32)
        d = (d0[pl.ds(x0, 4), lo - 1 : hi - 1] - centre) * inv_radius
        if prev is None:
            res = acc * (inv_radius / 72.0) + d * v
        else:
            res = acc * (inv_radius / 36.0) + (2.0 * d) * v - prev[px, lo:hi].astype(F32)
        out[px, lo:hi] = res.astype(BF16)

    def apply_step(u, prev, out, lo, hi):
        @pl.loop(0, 4, unroll=4)
        def _(i):
            apply_chunk(u, prev, out, 4 * i, lo, hi)

    def outside_zero(out):
        @pl.when(yy == 0)
        def _():
            out[:, 1] = jnp.zeros((18, 16, 256), BF16)

        @pl.when(yy == 3)
        def _():
            out[:, 10] = jnp.zeros((18, 16, 256), BF16)

    apply_step(u0, None, u1, 3, 9)
    apply_step(u1, u0, u2, 4, 8)

    def halo_wait(side):
        bulk(u0.at[1:17, 2], hal_r.at[side]).wait_recv()
        pot_edge(side).wait_recv()

    @pl.when(yy < 3)
    def _():
        halo_wait(0)

    @pl.when(yy > 0)
    def _():
        halo_wait(1)

    apply_step(u0, None, u1, 1, 3)
    apply_step(u0, None, u1, 9, 11)
    outside_zero(u1)
    apply_step(u1, u0, u2, 1, 4)
    apply_step(u1, u0, u2, 8, 11)
    outside_zero(u2)
    apply_step(u2, u1, u3, 1, 11)
    outside_zero(u3)
    def send_out(ks):
        for k in ks:
            px, p4 = peer(k)
            remote(
                u4.at[pl.ds(1 + 2 * px, 2), pl.ds(2 + 2 * p4, 2)],
                rf.at[j], f_s.at[0], f_r.at[0], (px, yy * 4 + p4),
            ).start()

    far_order = (*OTHER, *PLANE, *FIRST)
    for h, parity in ((1 - xl, 1), (xl, 0)):
        for i in range(2):
            apply_chunk(u3, u2, u4, 8 * h + 4 * i, 2, 10)
        send_out([k for k in far_order if (k // 4) % 2 == parity])

    def layer(side):
        far = rem(yy + 3 + 2 * side, 4)
        mine, theirs, lanes = (2, 10, pl.ds(0, 128)) if side == 0 else (9, 1, pl.ds(128, 128))
        return remote(
            u4.at[pl.ds(1, 16), mine, :, lanes],
            u4.at[pl.ds(1, 16), theirs, :, lanes],
            edge_s.at[side], edge_r.at[side], (sx, far * 4 + s4),
        )

    @pl.when(yy > 0)
    def _():
        layer(0).start()

    @pl.when(yy < 3)
    def _():
        layer(1).start()

    rf[j] = u4[xs, bs]

    @pl.when(yy < 3)
    def _():
        layer(0).wait_recv()

    @pl.when(yy > 0)
    def _():
        layer(1).wait_recv()

    zero = jnp.zeros((), BF16)

    @pl.loop(0, 2)
    def _(i):
        own, slab_p, slab_q, even_p, even_q = [], [], [], [], []
        first = lax.broadcasted_iota(jnp.int32, (8, 16, 128), 2) < 64
        last = lax.broadcasted_iota(jnp.int32, (8, 16, 128), 0) % 2 == 1
        for m in range(4):
            before, here, after = (u4.at[8 * i + 2 * m + n] for n in (1, 2, 3))
            own.append(after[2:10].reshape(128, 256))
            nxt = [u[3:11, :, 0:128] for u in (before, here, after)]
            slab_p.append(jnp.where(first & last, nxt[1], zero).reshape(128, 128))
            far = nxt[2] + jnp.where(last, nxt[0], zero)
            slab_q.append(jnp.where(first, far, after[1:9, :, 128:256]).reshape(128, 128))
            for b in (4, 6, 8, 10):
                even_p.append(jnp.where(first[0], before[b, :, 0:128], zero))
                even_q.append(jnp.where(first[0], here[b, :, 0:128], zero))
        join = lambda parts: jnp.concatenate(parts, axis=0)
        lhs = jnp.concatenate([join(own), join(slab_p), join(slab_q)], axis=1)
        acc = jnp.dot(lhs, w_in[256:768], preferred_element_type=F32) * (1.0 / 72.0)
        odd = acc.astype(BF16).reshape(4, 4, 2, 16, 256)
        for n in range(4):
            face[pl.ds(4 * i, 4), :, n] = odd[:, :, n // 2, :, 128 * (n % 2) : 128 * (n % 2) + 128]
        lhs = jnp.concatenate([join(even_p), join(even_q)], axis=1)
        acc = jnp.dot(lhs, w_in[512:768, 128:256], preferred_element_type=F32) * (1.0 / 72.0)
        face[pl.ds(4 * i, 4), :, 4] = acc.astype(BF16).reshape(4, 4, 16, 128)

    for k in (*OTHER, *PLANE, *FIRST):
        px, p4 = peer(k)
        dev = (px, yy * 4 + p4)
        remote(face.at[px, p4], faces.at[j], i_s.at[0], i_r.at[0], dev).start()
    faces[j] = face[sx, s4]

    units = [(a, b) for a in range(2) for b in range(2)]

    def flat(value):
        return value.reshape(-1, value.shape[-1])

    def core_copy(n, r):
        return remote(
            part.at[n, r, :, 1 - c], other.at[n, r], core_s.at[n, r], core_r.at[n, r], sibling
        )

    def give(n, r, g):
        g = g.reshape(2, 2, 2, 16, 512)
        gm[n, r] = g
        part[n, r] = g.astype(BF16)
        core_copy(n, r).start()

    def take(n, r):
        core_copy(n, r).wait_recv()
        half[n, r] = (gm[n, r, :, c] + other[n, r].astype(F32)).astype(BF16)

    def local_image():
        first = lax.broadcasted_iota(jnp.int32, (512, 128), 1) < 64
        for a, b in units:
            slabs = [flat(rf[:, n, b]) for n in (a, 1 - a)]
            for n in (a, 1 - a):
                if b == 0:
                    slabs.append(jnp.where(first, flat(rf[:, n, 1, :, 0:128]), zero))
                else:
                    slabs.append(jnp.where(first, zero, flat(rf[:, n, 0, :, 128:256])))
            acc = jnp.dot(jnp.concatenate(slabs, axis=1), w_in[...], preferred_element_type=F32)
            here = d0[2 * sx + a, 1 + 2 * s4 + b] * flat(rf[:, a, b]).astype(F32)
            ri[a, b] = (acc * (1.0 / 72.0) + here).astype(BF16)

    def nt(left, right):
        left, right = (jnp.concatenate(parts, axis=1) for parts in (left, right))
        return lax.dot_general(left, right, NT, preferred_element_type=F32)

    lanes_z = pl.ds(pl.multiple_of(128 * z, 128), 128)

    def margin_y_copy(dy):
        return remote(half.at[0, ys[dy]], ysum.at[dy], y_s.at[0], y_r.at[0], (sx, ys[dy] * 4 + s4))

    def margin_y_sum():
        total = half[0, yy].astype(F32)
        for dy in (1, 2, 3):
            total += ysum[dy].astype(F32)
        plane_part[...] = total.astype(BF16)

    def margin_plane_copy(k):
        dz, dx = k % 4, k // 4
        lanes = pl.ds(pl.multiple_of(128 * zs[dz], 128), 128)
        return remote(
            plane_part.at[xhs[dx], xls[dx], :, lanes], rs.at[0, k], rs_s.at[0], rs_r.at[0],
            (xls[dx] * 4 + zs[dz], yy * 4 + xhs[dx] * 2 + c),
        )

    def projected_copies(r, own):
        for k in (*PLANE, *FIRST) if own else (*PLANE, *FIRST, 0):
            dz, dx = k % 4, k // 4
            lanes = pl.ds(pl.multiple_of(128 * zs[dz], 128), 128)
            remote(
                half.at[1, r, xhs[dx], xls[dx], :, lanes],
                rs.at[1, 16 * yy + 4 * x + z], rs_s.at[1], rs_r.at[1],
                (xls[dx] * 4 + zs[dz], r * 4 + xhs[dx] * 2 + c),
            ).start()

    bulk(t.at[1:GROUP], f_r.at[0]).wait_recv()
    field_rows = [flat(rf[:, a, b]) for a, b in units]
    for r in range(4):
        give(0, r, nt([v[128 * r : 128 * r + 128] for v in field_rows], field_rows))
    local_image()
    for r in range(4):
        take(0, r)
    for dy in (1, 2, 3):
        margin_y_copy(dy).start()
    for r in range(4):
        gm[1, r] = nt(
            [v[128 * r : 128 * r + 128] for v in field_rows], [ri[a, b] for a, b in units]
        ).reshape(2, 2, 2, 16, 512)
    bulk(faces.at[1:GROUP], i_r.at[0]).wait_recv()
    order = [rem(yy + i, 4) for i in (2, 1, 3, 0)]
    def field(js):
        return [flat(v) for v in (rf[js, 1, 0], rf[js, 1, 1], rf[js, 0, 1, :, 128:256])]

    def across(js):
        return [flat(faces[js, n]) for n in range(5)]

    every = slice(None)
    right = across(every) + field(every)
    for r in order:
        eight = pl.ds(8 * r, 8)
        give(1, r, nt(field(eight) + across(eight), right) + gm[1, r].reshape(128, 512))
    for r in order:
        take(1, r)
        projected_copies(r, r is order[3])
    rs[1, 16 * yy + 4 * x + z] = half[1, yy, xh, xl, :, lanes_z]

    bulk(ysum.at[1:4], y_r.at[0]).wait_recv()
    margin_y_sum()
    for k in range(1, 16):
        margin_plane_copy(k).start()
    rs[0, 0] = plane_part[xh, xl, :, lanes_z]

    bulk(rs.at[0, 1:16], rs_r.at[0]).wait_recv()
    ob[sx, 0] = jnp.sum(rs[0, 0:16].astype(F32), axis=0)
    bulk(rs.at[1, 0:63], rs_r.at[1]).wait_recv()
    ob[sx, 1] = jnp.sum(rs[1].astype(F32), axis=0)

    for k in range(1, 8):
        far = rem(sx + k, 8)
        remote(ob.at[sx], ob.at[sx], ag_s.at[0], ag_r.at[0], (far, sy)).start()

    for sem in (in_s, f_s):
        bulk(t.at[1:GROUP], sem.at[0]).wait_send()
    bulk(faces.at[1:GROUP], i_s.at[0]).wait_send()
    for stage, n in enumerate((3, 12, 16)):
        bulk(rs.at[0, 0:n], pin_s.at[stage]).wait_send()

    def sent(side):
        bulk(u0.at[1:17, 2], hal_s.at[side]).wait_send()
        pot_edge(side).wait_send()
        layer(side).wait_send()

    @pl.when(yy > 0)
    def _():
        sent(0)

    @pl.when(yy < 3)
    def _():
        sent(1)

    for r in range(4):
        core_copy(0, r).wait_send()
        core_copy(1, r).wait_send()
    bulk(ysum.at[1:4], y_s.at[0]).wait_send()
    bulk(rs.at[0, 1:16], rs_s.at[0]).wait_send()
    bulk(rs.at[1, 0:63], rs_s.at[1]).wait_send()
    bulk(ob.at[0:7], ag_s.at[0]).wait_send()
    bulk(ob.at[0:7], ag_r.at[0]).wait_recv()
    for s in range(8):
        rows, lanes = pl.ds(16 * (s // 4), 16), pl.ds(128 * (s % 4), 128)
        summed[0, rows, lanes] = ob[s, 0]
        summed[1, rows, lanes] = ob[s, 1]


def on_device(wave, potential, lower_cut, upper_edge):
    dma = pltpu.SemaphoreType.DMA
    field = pltpu.VMEM((18, 12, 16, 256), BF16)
    block = pltpu.VMEM((GROUP, 2, 2, 16, 256), BF16)
    vmem = pl.BlockSpec(memory_space=pltpu.VMEM)
    hbm = pl.BlockSpec(memory_space=pl.ANY)
    smem = pl.BlockSpec(memory_space=pltpu.SMEM)
    weights = jnp.asarray(stencil_matrix(), BF16)
    summed = pl.pallas_call(
        kernel,
        out_shape=jax.ShapeDtypeStruct((2, 32, 512), F32),
        in_specs=[hbm, hbm, smem, smem, hbm],
        out_specs=vmem,
        scratch_shapes=[
            pltpu.VMEM(wave.shape, BF16),
            pltpu.VMEM(potential.shape, F32),
            pltpu.VMEM(weights.shape, BF16),
            block,
            field, field, field, field, field,
            pltpu.VMEM((8, 4, 5, 16, 128), BF16),
            pltpu.VMEM((16, 10, 1, 256), F32),
            block,
            pltpu.VMEM((GROUP, 5, 16, 128), BF16),
            pltpu.VMEM((2, 2, 512, 256), BF16),
            pltpu.VMEM((2, 4, 2, 2, 2, 16, 512), F32),
            pltpu.VMEM((2, 4, 2, 2, 2, 16, 512), BF16),
            pltpu.VMEM((2, 4, 2, 2, 16, 512), BF16),
            pltpu.VMEM((2, 4, 2, 2, 16, 512), BF16),
            pltpu.VMEM((4, 2, 2, 16, 512), BF16),
            pltpu.VMEM((2, 2, 16, 512), BF16),
            pltpu.VMEM((2, 64, 16, 128), BF16),
            pltpu.VMEM((8, 2, 16, 128), F32),
            dma((3,)), dma((1,)), dma((32,)), dma((3,)), dma((3,)),
            dma((2,)), dma((2,)), dma((2,)), dma((2,)),
            dma((2,)), dma((2,)),
            dma((1,)), dma((1,)), dma((1,)), dma((1,)),
            dma((2, 4)), dma((2, 4)), dma((1,)), dma((1,)), dma((2,)), dma((2,)),
            dma((1,)), dma((1,)),
            pltpu.SemaphoreType.REGULAR, pltpu.SemaphoreType.REGULAR,
        ],
        compiler_params=pltpu.CompilerParams(
            collective_id=0, has_side_effects=True, vmem_limit_bytes=127 << 19
        ),
    )(wave, potential, lower_cut, upper_edge, weights)
    return summed[0] * (1.0 / 131072.0), summed[1] * (1.0 / 131072.0)


def solution(mesh):
    return jax.shard_map(
        on_device,
        mesh=mesh,
        in_specs=(P("sx", "sy", None, None), P("sx", "sy", None), P(), P()),
        out_specs=(P("sy", None), P("sy", None)),
        check_vma=False,
    )
```

```python
import functools

import jax
import jax.numpy as jnp
import numpy as np
from jax import lax
from jax.experimental import pallas as pl
from jax.experimental.pallas import tpu as pltpu
from jax.sharding import PartitionSpec as P

MESH = pl.DeviceIdType.MESH
F32, BF16 = jnp.float32, jnp.bfloat16
GROUP = 32
FIRST = (2, 8, 1, 3, 4, 12)
PLANE = (10, 6, 14, 9, 11, 5, 7, 13, 15)
OTHER = (26, 22, 30, 25, 27, 18, 24, 21, 23, 29, 31, 17, 19, 20, 28, 16)
NT = (((1,), (1,)), ((), ()))


def stencil_matrix():
    my, ky = np.zeros((4, 6)), np.zeros((4, 6))
    for i in range(4):
        my[i, i : i + 3] = 1, 4, 1
        ky[i, i : i + 3] = -1, 2, -1
    mz, kz = np.zeros((64, 64)), np.zeros((64, 64))
    for i in range(64):
        for j in range(max(i - 1, 0), min(i + 2, 64)):
            mz[i, j] = 4 if i == j else 1
            kz[i, j] = 2 if i == j else -1
    m = np.einsum("ij,kl->jlik", my, mz).reshape(6, 64, 256)
    g = np.einsum("ij,kl->jlik", ky, mz) + np.einsum("ij,kl->jlik", my, kz)
    g = g.reshape(6, 64, 256)
    p, q = 2 * m + 4 * g, g - m
    own = lambda t: t[1:5].reshape(256, 256)
    edge = lambda t: np.concatenate([t[5], t[0]], axis=0)
    return np.concatenate([own(p), own(q), edge(p), edge(q)], axis=0)


def kernel(
    wave_hbm, pot_hbm, low, high, w_hbm, summed,
    wave, pot, w_in, t, u0, u1, u2, u3, u4, face, d0, rf, faces, ri, gm, part, other, half, ysum, plane_part, rs, ob,
    load, in_s, in_r, pin_s, pin_r, hal_s, hal_r, phal_s, phal_r, edge_s, edge_r,
    f_s, f_r, i_s, i_r, core_s, core_r, y_s, y_r, rs_s, rs_r, ag_s, ag_r, plane, chip,
):
    loads = [
        pltpu.make_async_copy(src, dst, load.at[i])
        for i, (src, dst) in enumerate([(wave_hbm, wave), (pot_hbm, pot), (w_hbm, w_in)])
    ]
    for copy in loads:
        copy.start()

    sx, sy = lax.axis_index("sx"), lax.axis_index("sy")
    rem, div = lax.rem, lax.div
    xl, z, yy, s4 = div(sx, 4), rem(sx, 4), div(sy, 4), rem(sy, 4)
    xh, c = div(s4, 2), rem(s4, 2)
    x = 2 * xh + xl
    j = sx * 4 + s4

    turn = [None, 1 + 2 * c, 2, 3 - 2 * c]
    zs = [z] + [rem(z + turn[d], 4) for d in (1, 2, 3)]
    xt = [x] + [rem(x + turn[d], 4) for d in (1, 2, 3)]
    ys = [yy] + [rem(yy + turn[d], 4) for d in (1, 2, 3)]
    xls, xhs, cs = [rem(v, 2) for v in xt], [div(v, 2) for v in xt], [c, 1 - c]
    def peer(k):
        dz, dx, dc = k % 4, (k // 4) % 4, k // 16
        return xls[dx] * 4 + zs[dz], xhs[dx] * 2 + cs[dc]

    def remote(src, dst, ss, rr, dev):
        return pltpu.make_async_remote_copy(
            src_ref=src, dst_ref=dst, send_sem=ss, recv_sem=rr, device_id=dev, device_id_type=MESH
        )

    sibling = (sx, sy + 1 - 2 * c)

    def bulk(ref, sem):
        return remote(ref, ref, sem, sem, sibling)

    for u in (u0, u1, u2, u3, u4):
        u[0] = jnp.zeros(u.shape[1:], BF16)
        u[17] = jnp.zeros(u.shape[1:], BF16)
        for b in (0, 1, 10, 11):
            u[:, b] = jnp.zeros((18, 16, 256), BF16)
    d0[:, 0] = jnp.zeros((16, 1, 256), F32)
    d0[:, 9] = jnp.zeros((16, 1, 256), F32)

    barrier = pltpu.get_barrier_semaphore()
    direct = [(px, yy * 4 + p4) for px, p4 in (peer(k) for k in (1, 2, 3, 4, 8, 12, 16))]
    direct += [(sx, ys[dy] * 4 + s4) for dy in (1, 2, 3)]
    for dev in direct:
        pl.semaphore_signal(barrier, inc=1, device_id=dev, device_id_type=MESH)

    eye = (
        lax.broadcasted_iota(jnp.int32, (256, 256), 0)
        == lax.broadcasted_iota(jnp.int32, (256, 256), 1)
    ).astype(F32).astype(BF16)
    loads[0].wait()
    loads[1].wait()
    for a in range(2):
        for b in range(2):
            nodes = wave[a, 4 * b : 4 * b + 4].reshape(256, 512)
            for h in range(2):
                turned = lax.dot_general(
                    eye, nodes[:, 256 * h : 256 * h + 256], NT, preferred_element_type=F32
                )
                t[16 * h : 16 * h + 16, a, b] = turned.astype(BF16).reshape(16, 16, 256)
            d0[2 * sx + a, 1 + 2 * s4 + b] = jnp.concatenate(
                [pot[a, 4 * b + i : 4 * b + i + 1, :] for i in range(4)], axis=1
            )

    pl.semaphore_wait(barrier, len(direct))

    xs = pl.ds(1 + 2 * sx, 2)
    bs = pl.ds(2 + 2 * s4, 2)
    own_pot = d0.at[pl.ds(2 * sx, 2), pl.ds(1 + 2 * s4, 2)]

    has_edge = 1 - (xh + c - 2 * xh * c)
    in_slot = has_edge * (2 * sx + c) + (1 - has_edge) * 16

    def in_copy(k):
        px, p4 = peer(k)
        return remote(
            t.at[px * 4 + p4], u0.at[xs, bs], in_s.at[0], in_r.at[in_slot], (px, yy * 4 + p4)
        )

    def send_in(ks):
        for k in ks:
            in_copy(k).start()

    def send_pot(strip, stage, devs):
        for dev in devs:
            remote(strip, strip, pin_s.at[stage], pin_r.at[stage], dev).start()

    along_z, along_x = direct[0:3], direct[3:6]
    for dev in along_z:
        pl.semaphore_signal(plane, inc=1, device_id=dev, device_id_type=MESH)
    send_pot(own_pot, 0, along_z)
    send_in(FIRST)
    pl.semaphore_wait(plane, 3)
    pl.semaphore_signal(chip, inc=1, device_id=sibling, device_id_type=MESH)
    bulk(rs.at[0, 0:3], pin_r.at[0]).wait_recv()
    send_pot(d0.at[pl.ds(8 * xl, 8), pl.ds(1 + 2 * s4, 2)], 1, along_x)
    send_in(PLANE)
    pl.semaphore_wait(chip, 1)
    send_in(OTHER)
    bulk(rs.at[0, 0:12], pin_r.at[1]).wait_recv()
    for q in (c, 2 + c):
        send_pot(d0.at[:, pl.ds(1 + 2 * q, 2)], 2, [sibling])

    u0[xs, bs] = t[j]

    def edge_ends(side):
        far = rem(yy + 3 + 2 * side, 4)
        return ((2, 10) if side == 0 else (9, 1)) + ((sx, far * 4 + s4),)

    def send_on(s, quarter):
        side = quarter // 3
        mine, theirs, dev = edge_ends(side)
        ux = pl.ds(1 + 2 * s, 2)

        @pl.when(yy > 0 if side == 0 else yy < 3)
        def _():
            remote(u0.at[ux, mine], u0.at[ux, theirs], hal_s.at[side], hal_r.at[side], dev).start()

    def pot_edge(side):
        mine, theirs, dev = edge_ends(side)
        return remote(
            d0.at[:, mine - 1], d0.at[:, theirs - 1], phal_s.at[side], phal_r.at[side], dev
        )

    bulk(rs.at[0, 0:16], pin_r.at[2]).wait_recv()

    @pl.when(yy > 0)
    def _():
        pot_edge(0).start()

    @pl.when(yy < 3)
    def _():
        pot_edge(1).start()

    for s in range(8):
        for quarter in (0, 3):

            @pl.when(j != 4 * s + quarter)
            def _():
                bulk(u0.at[xs, bs], in_r.at[2 * s + quarter // 3]).wait_recv()

            send_on(s, quarter)

    @pl.when(has_edge == 1)
    def _():
        bulk(t.at[0:16], in_r.at[16]).wait_recv()

    @pl.when(has_edge == 0)
    def _():
        bulk(t.at[0:15], in_r.at[16]).wait_recv()

    loads[2].wait()
    centre = 0.5 * (high[0] + low[0])
    inv_radius = 1.0 / (0.5 * (high[0] - low[0]))

    def edge_slab(nxt, prv):
        return jnp.where(lax.broadcasted_iota(jnp.int32, nxt.shape, len(nxt.shape) - 1) < 64, nxt, prv)

    def stencil(u, x0, lo, hi):
        n = hi - lo
        rows = 4 * n * 16
        mid = u[pl.ds(x0 + 1, 4), lo - 1 : hi + 1]
        beside = u[pl.ds(x0, 4), lo - 1 : hi + 1] + u[pl.ds(x0 + 2, 4), lo - 1 : hi + 1]
        slabs = [v[:, 1 : n + 1].reshape(rows, 256) for v in (mid, beside)]
        slabs += [
            edge_slab(v[:, 2:, :, 0:128], v[:, :n, :, 128:256]).reshape(rows, 128)
            for v in (mid, beside)
        ]
        acc = jnp.dot(jnp.concatenate(slabs, axis=1), w_in[...], preferred_element_type=F32)
        return acc.reshape(4, n, 16, 256)

    def apply_chunk(u, prev, out, x0, lo, hi):
        acc = stencil(u, x0, lo, hi)
        px = pl.ds(x0 + 1, 4)
        v = u[px, lo:hi].astype(F32)
        d = (d0[pl.ds(x0, 4), lo - 1 : hi - 1] - centre) * inv_radius
        if prev is None:
            res = acc * (inv_radius / 72.0) + d * v
        else:
            res = acc * (inv_radius / 36.0) + (2.0 * d) * v - prev[px, lo:hi].astype(F32)
        out[px, lo:hi] = res.astype(BF16)

    def apply_step(u, prev, out, lo, hi):
        @pl.loop(0, 4, unroll=4)
        def _(i):
            apply_chunk(u, prev, out, 4 * i, lo, hi)

    def outside_zero(out):
        @pl.when(yy == 0)
        def _():
            out[:, 1] = jnp.zeros((18, 16, 256), BF16)

        @pl.when(yy == 3)
        def _():
            out[:, 10] = jnp.zeros((18, 16, 256), BF16)

    apply_step(u0, None, u1, 3, 9)
    apply_step(u1, u0, u2, 4, 8)

    def halo_wait(side):
        bulk(u0.at[1:17, 2], hal_r.at[side]).wait_recv()
        pot_edge(side).wait_recv()

    @pl.when(yy < 3)
    def _():
        halo_wait(0)

    @pl.when(yy > 0)
    def _():
        halo_wait(1)

    apply_step(u0, None, u1, 1, 3)
    apply_step(u0, None, u1, 9, 11)
    outside_zero(u1)
    apply_step(u1, u0, u2, 1, 4)
    apply_step(u1, u0, u2, 8, 11)
    outside_zero(u2)
    apply_step(u2, u1, u3, 1, 11)
    outside_zero(u3)
    def send_out(ks):
        for k in ks:
            px, p4 = peer(k)
            remote(
                u4.at[pl.ds(1 + 2 * px, 2), pl.ds(2 + 2 * p4, 2)],
                rf.at[j], f_s.at[0], f_r.at[0], (px, yy * 4 + p4),
            ).start()

    far_order = (*OTHER, *PLANE, *FIRST)
    for h, parity in ((1 - xl, 1), (xl, 0)):
        for i in range(2):
            apply_chunk(u3, u2, u4, 8 * h + 4 * i, 2, 10)
        send_out([k for k in far_order if (k // 4) % 2 == parity])

    def layer(side):
        far = rem(yy + 3 + 2 * side, 4)
        mine, theirs, lanes = (2, 10, pl.ds(0, 128)) if side == 0 else (9, 1, pl.ds(128, 128))
        return remote(
            u4.at[pl.ds(1, 16), mine, :, lanes],
            u4.at[pl.ds(1, 16), theirs, :, lanes],
            edge_s.at[side], edge_r.at[side], (sx, far * 4 + s4),
        )

    @pl.when(yy > 0)
    def _():
        layer(0).start()

    @pl.when(yy < 3)
    def _():
        layer(1).start()

    rf[j] = u4[xs, bs]

    @pl.when(yy < 3)
    def _():
        layer(0).wait_recv()

    @pl.when(yy > 0)
    def _():
        layer(1).wait_recv()

    zero = jnp.zeros((), BF16)

    @pl.loop(0, 2)
    def _(i):
        own, slab_p, slab_q, even_p, even_q = [], [], [], [], []
        first = lax.broadcasted_iota(jnp.int32, (8, 16, 128), 2) < 64
        last = lax.broadcasted_iota(jnp.int32, (8, 16, 128), 0) % 2 == 1
        for m in range(4):
            before, here, after = (u4.at[8 * i + 2 * m + n] for n in (1, 2, 3))
            own.append(after[2:10].reshape(128, 256))
            nxt = [u[3:11, :, 0:128] for u in (before, here, after)]
            slab_p.append(jnp.where(first & last, nxt[1], zero).reshape(128, 128))
            far = nxt[2] + jnp.where(last, nxt[0], zero)
            slab_q.append(jnp.where(first, far, after[1:9, :, 128:256]).reshape(128, 128))
            for b in (4, 6, 8, 10):
                even_p.append(jnp.where(first[0], before[b, :, 0:128], zero))
                even_q.append(jnp.where(first[0], here[b, :, 0:128], zero))
        join = lambda parts: jnp.concatenate(parts, axis=0)
        lhs = jnp.concatenate([join(own), join(slab_p), join(slab_q)], axis=1)
        acc = jnp.dot(lhs, w_in[256:768], preferred_element_type=F32) * (1.0 / 72.0)
        odd = acc.astype(BF16).reshape(4, 4, 2, 16, 256)
        for n in range(4):
            face[pl.ds(4 * i, 4), :, n] = odd[:, :, n // 2, :, 128 * (n % 2) : 128 * (n % 2) + 128]
        lhs = jnp.concatenate([join(even_p), join(even_q)], axis=1)
        acc = jnp.dot(lhs, w_in[512:768, 128:256], preferred_element_type=F32) * (1.0 / 72.0)
        face[pl.ds(4 * i, 4), :, 4] = acc.astype(BF16).reshape(4, 4, 16, 128)

    for k in (*OTHER, *PLANE, *FIRST):
        px, p4 = peer(k)
        dev = (px, yy * 4 + p4)
        remote(face.at[px, p4], faces.at[j], i_s.at[0], i_r.at[0], dev).start()
    faces[j] = face[sx, s4]

    units = [(a, b) for a in range(2) for b in range(2)]

    def flat(value):
        return value.reshape(-1, value.shape[-1])

    def core_copy(n, r):
        return remote(
            part.at[n, r, :, 1 - c], other.at[n, r], core_s.at[n], core_r.at[n, r], sibling
        )

    def give(n, r, g):
        g = g.reshape(2, 2, 2, 16, 512)
        gm[n, r] = g
        part[n, r] = g.astype(BF16)
        core_copy(n, r).start()

    def take(n, r):
        core_copy(n, r).wait_recv()
        half[n, r] = (gm[n, r, :, c] + other[n, r].astype(F32)).astype(BF16)

    def local_image():
        first = lax.broadcasted_iota(jnp.int32, (512, 128), 1) < 64
        for a, b in units:
            slabs = [flat(rf[:, n, b]) for n in (a, 1 - a)]
            for n in (a, 1 - a):
                if b == 0:
                    slabs.append(jnp.where(first, flat(rf[:, n, 1, :, 0:128]), zero))
                else:
                    slabs.append(jnp.where(first, zero, flat(rf[:, n, 0, :, 128:256])))
            acc = jnp.dot(jnp.concatenate(slabs, axis=1), w_in[...], preferred_element_type=F32)
            here = d0[2 * sx + a, 1 + 2 * s4 + b] * flat(rf[:, a, b]).astype(F32)
            ri[a, b] = (acc * (1.0 / 72.0) + here).astype(BF16)

    def nt(left, right):
        left, right = (jnp.concatenate(parts, axis=1) for parts in (left, right))
        return lax.dot_general(left, right, NT, preferred_element_type=F32)

    lanes_z = pl.ds(pl.multiple_of(128 * z, 128), 128)

    def margin_y_copy(dy):
        return remote(half.at[0, ys[dy]], ysum.at[dy], y_s.at[0], y_r.at[0], (sx, ys[dy] * 4 + s4))

    def margin_y_sum():
        total = half[0, yy].astype(F32)
        for dy in (1, 2, 3):
            total += ysum[dy].astype(F32)
        plane_part[...] = total.astype(BF16)

    def margin_plane_copy(k):
        dz, dx = k % 4, k // 4
        lanes = pl.ds(pl.multiple_of(128 * zs[dz], 128), 128)
        return remote(
            plane_part.at[xhs[dx], xls[dx], :, lanes], rs.at[0, k], rs_s.at[0], rs_r.at[0],
            (xls[dx] * 4 + zs[dz], yy * 4 + xhs[dx] * 2 + c),
        )

    def projected_copies(r, own):
        for k in (*PLANE, *FIRST) if own else (*PLANE, *FIRST, 0):
            dz, dx = k % 4, k // 4
            lanes = pl.ds(pl.multiple_of(128 * zs[dz], 128), 128)
            remote(
                half.at[1, r, xhs[dx], xls[dx], :, lanes],
                rs.at[1, 16 * yy + 4 * x + z], rs_s.at[1], rs_r.at[1],
                (xls[dx] * 4 + zs[dz], r * 4 + xhs[dx] * 2 + c),
            ).start()

    bulk(t.at[1:GROUP], f_r.at[0]).wait_recv()
    field_rows = [flat(rf[:, a, b]) for a, b in units]
    for r in range(4):
        give(0, r, nt([v[128 * r : 128 * r + 128] for v in field_rows], field_rows))
    local_image()
    for r in range(4):
        take(0, r)
    for dy in (1, 2, 3):
        margin_y_copy(dy).start()
    for r in range(4):
        gm[1, r] = nt(
            [v[128 * r : 128 * r + 128] for v in field_rows], [ri[a, b] for a, b in units]
        ).reshape(2, 2, 2, 16, 512)
    bulk(faces.at[1:GROUP], i_r.at[0]).wait_recv()
    order = [rem(yy + i, 4) for i in (2, 1, 3, 0)]
    def field(js):
        return [flat(v) for v in (rf[js, 1, 0], rf[js, 1, 1], rf[js, 0, 1, :, 128:256])]

    def across(js):
        return [flat(faces[js, n]) for n in range(5)]

    every = slice(None)
    right = across(every) + field(every)
    for r in order:
        eight = pl.ds(8 * r, 8)
        give(1, r, nt(field(eight) + across(eight), right) + gm[1, r].reshape(128, 512))
    for r in order:
        take(1, r)
        projected_copies(r, r is order[3])
    rs[1, 16 * yy + 4 * x + z] = half[1, yy, xh, xl, :, lanes_z]

    bulk(ysum.at[1:4], y_r.at[0]).wait_recv()
    margin_y_sum()
    for k in range(1, 16):
        margin_plane_copy(k).start()
    rs[0, 0] = plane_part[xh, xl, :, lanes_z]

    bulk(rs.at[0, 1:16], rs_r.at[0]).wait_recv()
    ob[sx, 0] = jnp.sum(rs[0, 0:16].astype(F32), axis=0)
    bulk(rs.at[1, 0:63], rs_r.at[1]).wait_recv()
    ob[sx, 1] = jnp.sum(rs[1].astype(F32), axis=0)

    for k in range(1, 8):
        far = rem(sx + k, 8)
        remote(ob.at[sx], ob.at[sx], ag_s.at[0], ag_r.at[0], (far, sy)).start()

    for sem in (in_s, f_s):
        bulk(t.at[1:GROUP], sem.at[0]).wait_send()
    bulk(faces.at[1:GROUP], i_s.at[0]).wait_send()
    for stage, n in enumerate((3, 12, 16)):
        bulk(rs.at[0, 0:n], pin_s.at[stage]).wait_send()

    def sent(side):
        bulk(u0.at[1:17, 2], hal_s.at[side]).wait_send()
        pot_edge(side).wait_send()
        layer(side).wait_send()

    @pl.when(yy > 0)
    def _():
        sent(0)

    @pl.when(yy < 3)
    def _():
        sent(1)

    for n in range(2):
        bulk(other.at[n], core_s.at[n]).wait_send()
    bulk(ysum.at[1:4], y_s.at[0]).wait_send()
    bulk(rs.at[0, 1:16], rs_s.at[0]).wait_send()
    bulk(rs.at[1, 0:63], rs_s.at[1]).wait_send()
    bulk(ob.at[0:7], ag_s.at[0]).wait_send()
    bulk(ob.at[0:7], ag_r.at[0]).wait_recv()
    for s in range(8):
        rows, lanes = pl.ds(16 * (s // 4), 16), pl.ds(128 * (s % 4), 128)
        summed[0, rows, lanes] = ob[s, 0]
        summed[1, rows, lanes] = ob[s, 1]


def on_device(wave, potential, lower_cut, upper_edge):
    dma = pltpu.SemaphoreType.DMA
    field = pltpu.VMEM((18, 12, 16, 256), BF16)
    block = pltpu.VMEM((GROUP, 2, 2, 16, 256), BF16)
    vmem = pl.BlockSpec(memory_space=pltpu.VMEM)
    hbm = pl.BlockSpec(memory_space=pl.ANY)
    smem = pl.BlockSpec(memory_space=pltpu.SMEM)
    weights = jnp.asarray(stencil_matrix(), BF16)
    summed = pl.pallas_call(
        kernel,
        out_shape=jax.ShapeDtypeStruct((2, 32, 512), F32),
        in_specs=[hbm, hbm, smem, smem, hbm],
        out_specs=vmem,
        scratch_shapes=[
            pltpu.VMEM(wave.shape, BF16),
            pltpu.VMEM(potential.shape, F32),
            pltpu.VMEM(weights.shape, BF16),
            block,
            field, field, field, field, field,
            pltpu.VMEM((8, 4, 5, 16, 128), BF16),
            pltpu.VMEM((16, 10, 1, 256), F32),
            block,
            pltpu.VMEM((GROUP, 5, 16, 128), BF16),
            pltpu.VMEM((2, 2, 512, 256), BF16),
            pltpu.VMEM((2, 4, 2, 2, 2, 16, 512), F32),
            pltpu.VMEM((2, 4, 2, 2, 2, 16, 512), BF16),
            pltpu.VMEM((2, 4, 2, 2, 16, 512), BF16),
            pltpu.VMEM((2, 4, 2, 2, 16, 512), BF16),
            pltpu.VMEM((4, 2, 2, 16, 512), BF16),
            pltpu.VMEM((2, 2, 16, 512), BF16),
            pltpu.VMEM((2, 64, 16, 128), BF16),
            pltpu.VMEM((8, 2, 16, 128), F32),
            dma((3,)), dma((1,)), dma((17,)), dma((3,)), dma((3,)),
            dma((2,)), dma((2,)), dma((2,)), dma((2,)),
            dma((2,)), dma((2,)),
            dma((1,)), dma((1,)), dma((1,)), dma((1,)),
            dma((2,)), dma((2, 4)), dma((1,)), dma((1,)), dma((2,)), dma((2,)),
            dma((1,)), dma((1,)),
            pltpu.SemaphoreType.REGULAR, pltpu.SemaphoreType.REGULAR,
        ],
        compiler_params=pltpu.CompilerParams(
            collective_id=0, has_side_effects=True, vmem_limit_bytes=127 << 19
        ),
    )(wave, potential, lower_cut, upper_edge, weights)
    return summed[0] * (1.0 / 131072.0), summed[1] * (1.0 / 131072.0)


def solution(mesh):
    return jax.shard_map(
        on_device,
        mesh=mesh,
        in_specs=(P("sx", "sy", None, None), P("sx", "sy", None), P(), P()),
        out_specs=(P("sy", None), P("sy", None)),
        check_vma=False,
    )
```
